256 devices in a mesh: seq: 32 (over x, z_hi, y), chan: 8 (over z_lo, core).
Axes of the slice: x: 4, y: 4, z: 8 (z_hi: 2, z_lo: 4; z = z_hi * 4 + z_lo), core: 2. Of those that a mesh axis runs over, the one named last changes fastest.
Arguments:
- hyena_gate: bfloat16 [16384, 4096], P('seq', 'chan'), may hold values from -6 to 6
- hyena_key: bfloat16 [16384, 4096], P('seq', 'chan'), may hold values from -6 to 6
- hyena_value: bfloat16 [16384, 4096], P('seq', 'chan'), may hold values from -6 to 6
- long_filter: bfloat16 [16384, 4096], P('seq', 'chan'), may hold values from -0.046875 to 0.046875
- skip_weight: float32 [4096], P('chan'), may hold values from -4 to 4
- attn_query: bfloat16 [16384, 8, 1024], P('seq', 'chan'), may hold values from -4.5 to 4.5
- attn_keys: bfloat16 [16384, 1024], P('seq', 'chan'), may hold values from -4.5 to 4.5
- attn_values: bfloat16 [16384, 1024], P('seq', 'chan'), may hold values from -6 to 6
Outputs:
- hyena_out: bfloat16 [16384, 4096], P('seq', 'chan')
- attn_out: bfloat16 [16384, 8, 1024], P('seq', 'chan')
- attn_lse: float32 [8, 8, 16384], P('chan', None, 'seq')
The draws below stay inside these ranges and needn't reach their ends.
All inputs are finite; a program needn't handle non-finite values.
Results may differ from the reference program's by a relative error of at most 0.0045.
Values may be sent and summed in bfloat16 or wider, within the bound.
No kernel may reach another device: no remote copies, remote signals or barrier semaphores. Data moves between devices by JAX's collectives and lax.ppermute only.
A program may use at most 128 MiB of HBM per device.

```python
import math
import jax
import jax.numpy as jnp
from jax import lax

C = 4096
KVH = 8
GROUP = 8
HD = 128
TOK_DEV = 512
TOKENS = 16384
N_SEQ = 32


def draw_attn_query(key, part):
    key = jax.random.fold_in(key, 1)
    drawn = jnp.clip(jax.random.normal(key, (TOKENS, GROUP, KVH * HD), jnp.float32), -4.5, 4.5)
    return drawn.astype(jnp.bfloat16)


def draw_attn_keys(key, part):
    key = jax.random.fold_in(key, 2)
    drawn = jnp.clip(jax.random.normal(key, (TOKENS, KVH * HD), jnp.float32), -4.5, 4.5)
    return drawn.astype(jnp.bfloat16)


def shard_levels(rng, shape, split, low, largest):
    level, own = 1.0, jax.random.fold_in(rng, 6)
    for axis_at, parts in split:
        steps = jnp.exp(jax.random.uniform(jax.random.fold_in(own, axis_at), (parts,), jnp.float32, low / len(split), largest / len(split)))
        level = level * jnp.repeat(steps, shape[axis_at] // parts).reshape([-1 if axis == axis_at else 1 for axis in range(len(shape))])
    return level


def centred(key, extent, deviation, reach, cuts=(), held_as=jnp.bfloat16):
    values = deviation * jax.random.normal(key, extent, jnp.float32)
    if cuts:
        values = values * shard_levels(key, extent, cuts, -0.22, 0.18)
    return jnp.clip(values, -reach, reach).astype(held_as)


def setup_inputs(seed: int = 0) -> dict:
    seeds = jax.random.split(jax.random.key(seed), 9)
    return {
        "hyena_gate": centred(seeds[0], (TOKENS, C), 1.0, 6.0, ((0, 32), (1, 8))),
        "hyena_key": centred(seeds[1], (TOKENS, C), 1.0, 6.0, ((0, 32), (1, 8))),
        "hyena_value": centred(seeds[2], (TOKENS, C), 1.0, 6.0, ((0, 32), (1, 8))),
        "long_filter": centred(seeds[3], (TOKENS, C), TOKENS ** -0.5, 0.046875, ((0, 32), (1, 8))),
        "skip_weight": centred(seeds[4], (C,), 1.0, 4.0, ((0, 8),), jnp.float32),
        "attn_query": draw_attn_query(jax.random.fold_in(seeds[8], 71), 0),
        "attn_keys": draw_attn_keys(jax.random.fold_in(seeds[8], 71), 0),
        "attn_values": centred(seeds[7], (TOKENS, KVH * HD), 1.0, 6.0, ((0, 32), (1, 8))),
    }


def long_conv(signal, kernel):
    chan_block = math.gcd(C, 256)
    block_count = C // chan_block

    def regroup(array):
        return array.reshape(TOKENS, block_count, chan_block).transpose(1, 0, 2)

    def convolve(pieces):
        sig_block, ker_block = pieces
        fft_size = 2 * TOKENS
        product = jnp.fft.rfft(sig_block, n=fft_size, axis=0) * jnp.fft.rfft(ker_block, n=fft_size, axis=0)
        return jnp.fft.irfft(product, n=fft_size, axis=0)[:TOKENS]

    result = lax.map(convolve, (regroup(signal), regroup(kernel)))
    return result.transpose(1, 0, 2).reshape(TOKENS, C).astype(signal.dtype)


def attend(attn_query, attn_keys, attn_values):
    zeros = jnp.zeros((TOK_DEV, KVH * HD), jnp.bfloat16)
    key_pad = jnp.concatenate([zeros, attn_keys], axis=0)
    value_pad = jnp.concatenate([zeros, attn_values], axis=0)
    key_pos = jnp.arange(2 * TOK_DEV, dtype=jnp.int32) - TOK_DEV
    query_pos = jnp.arange(TOK_DEV, dtype=jnp.int32)

    def one_block(block_id):
        start = (block_id * TOK_DEV).astype(jnp.int32)
        queries = lax.dynamic_slice_in_dim(attn_query, start, TOK_DEV, 0).reshape(TOK_DEV, GROUP, KVH, HD)
        key_rows = lax.dynamic_slice_in_dim(key_pad, start, 2 * TOK_DEV, 0).reshape(2 * TOK_DEV, KVH, HD)
        value_rows = lax.dynamic_slice_in_dim(value_pad, start, 2 * TOK_DEV, 0).reshape(2 * TOK_DEV, KVH, HD)
        scores = jnp.einsum("tgjd,sjd->gjts", queries.astype(jnp.float32), key_rows.astype(jnp.float32)) * (HD ** -0.5)
        allowed = (key_pos[None, :] <= query_pos[:, None]) & ((key_pos[None, :] >= 0) | (block_id > 0))
        scores = jnp.where(allowed, scores, jnp.float32(-1e30))
        row_peak = jnp.max(scores, axis=-1)
        expd = jnp.exp(scores - row_peak[..., None])
        row_total = jnp.sum(expd, axis=-1)
        weights = expd.astype(jnp.bfloat16)
        mixed_sum = jnp.einsum("gjts,sjd->tgjd", weights.astype(jnp.float32), value_rows.astype(jnp.float32))
        normed = mixed_sum / row_total.transpose(2, 0, 1)[..., None]
        return normed.astype(jnp.bfloat16).reshape(TOK_DEV, GROUP, KVH * HD), row_peak + jnp.log(row_total)

    outputs, lse_blocks = lax.map(one_block, jnp.arange(N_SEQ, dtype=jnp.int32))
    attn_out = outputs.reshape(TOKENS, GROUP, KVH * HD)
    attn_lse = lse_blocks.transpose(1, 2, 0, 3).reshape(GROUP, KVH, TOKENS)
    return attn_out, attn_lse


def reference(hyena_gate, hyena_key, hyena_value, long_filter, skip_weight, attn_query, attn_keys, attn_values):
    signal = hyena_key.astype(jnp.float32) * hyena_value.astype(jnp.float32)
    kernel = long_filter.astype(jnp.float32)
    conv = long_conv(signal, kernel)
    hyena_out = (hyena_gate.astype(jnp.float32) * (conv + skip_weight * signal)).astype(jnp.bfloat16)
    attn_out, attn_lse = attend(attn_query, attn_keys, attn_values)
    return hyena_out, attn_out, attn_lse
```

```python
import functools
import math

import jax
import jax.numpy as jnp
import ml_dtypes
import numpy as np
from jax import lax
from jax.experimental import pallas as pl
from jax.experimental.pallas import tpu as pltpu
from jax.sharding import PartitionSpec as P

KVH = 8
HD = 128
TOK = 512
SEQ = 32
CHAN = 8
CH = 512
MINE = CH // SEQ
LINES = 128
COLS = 128
SIZE = 2 * LINES * COLS
BF = jnp.bfloat16
F32 = jnp.float32
MASKED = -1e30

ONES = (((1,), (1,)), ((), ()))
PLAIN = (((1,), (0,)), ((), ()))
FIRST = (((0,), (0,)), ((), ()))


def dot(a, b, dims=PLAIN):
    return lax.dot_general(a, b, dims, preferred_element_type=F32)


def split(x):
    high = x.astype(BF)
    return high, (x - high.astype(F32)).astype(BF)


def np_split(x):
    high = x.astype(ml_dtypes.bfloat16)
    low = (x - high.astype(np.float64)).astype(ml_dtypes.bfloat16)
    return high, low


def tables():
    rows = np.arange(LINES)
    line = 4 * (rows % SEQ) + rows // SEQ
    freq = np.arange(LINES) + 0.5
    angle = 2 * np.pi * np.outer(freq, line) / (2 * LINES)
    first = np.concatenate([np.cos(angle), -np.sin(angle)], axis=0)
    first_hi, first_lo = np_split(first)
    first_both = np.concatenate([first_hi, first_lo], axis=1)
    last_hi, last_lo = np_split(first.T * (2.0 / SIZE))
    turn = 2 * np.pi * np.outer(freq, np.arange(COLS)) / SIZE
    turn_cos, turn_sin = np.cos(turn).astype(np.float32), np.sin(turn).astype(np.float32)
    angle = 2 * np.pi * np.outer(np.arange(COLS), np.arange(COLS)) / COLS
    cos, sin = np.cos(angle), np.sin(angle)
    there = np.block([[cos, -sin], [sin, cos]])
    back = np.block([[cos, sin], [-sin, cos]])
    return (first_both, last_hi, last_lo, turn_cos, turn_sin, *np_split(there), *np_split(back))


def eye(n):
    at = lax.broadcasted_iota(jnp.int32, (n, n), 0) == lax.broadcasted_iota(jnp.int32, (n, n), 1)
    return at.astype(F32).astype(BF)


def turn_kernel(key_ref, value_ref, filter_ref, out_ref):
    unit = eye(256)
    for half in range(2):
        cols = slice(half * 256, half * 256 + 256)
        groups = slice(half * 16, half * 16 + 16)
        signal = (key_ref[:, cols].astype(F32) * value_ref[:, cols].astype(F32)).astype(BF)
        out_ref[groups, 0] = dot(unit, signal, ONES).astype(BF).reshape(16, MINE, TOK)
        out_ref[groups, 1] = dot(unit, filter_ref[:, cols], ONES).astype(BF).reshape(16, MINE, TOK)


def turn_call(key, value, long_filter):
    return pl.pallas_call(
        turn_kernel,
        out_shape=jax.ShapeDtypeStruct((SEQ, 2, MINE, TOK), BF),
        compiler_params=pltpu.CompilerParams(vmem_limit_bytes=32 * 2**20),
        cost_estimate=pl.CostEstimate(flops=2**29, bytes_accessed=5 * 2**19, transcendentals=0),
        name="turn",
    )(key, value, long_filter)


def conv_kernel(
    in_ref,
    first_ref,
    last_hi_ref,
    last_lo_ref,
    cos_ref,
    sin_ref,
    there_hi_ref,
    there_lo_ref,
    back_hi_ref,
    back_lo_ref,
    out_ref,
    wide,
    spec_hi,
    spec_lo,
    result,
):
    for which in range(2):
        for q in range(4):
            part = in_ref[:, which, :, q * 128 : q * 128 + 128].astype(F32)
            wide[which, q * 512 : q * 512 + 512, :] = part.reshape(512, 128)

    def spread(ch, carry):
        both = jnp.concatenate(
            [wide[which, pl.ds(ch, LINES, stride=MINE), :] for which in range(2)], axis=1
        ).astype(BF)
        both = jnp.concatenate([both, both], axis=0)
        lines = dot(first_ref[...], both)
        cos, sin = cos_ref[...], sin_ref[...]
        for which in range(2):
            re = lines[:LINES, which * COLS : which * COLS + COLS]
            im = lines[LINES:, which * COLS : which * COLS + COLS]
            turned = jnp.concatenate([re * cos + im * sin, im * cos - re * sin], axis=1)
            high, low = split(turned)
            rows = pl.ds(pl.multiple_of(ch * LINES, LINES), LINES)
            spec_hi[which, rows, :] = high
            spec_lo[which, rows, :] = low
        return carry

    lax.fori_loop(0, MINE, spread, 0, unroll=2)

    many = 4

    def multiply(step, carry):
        rows = pl.ds(pl.multiple_of(step * (many * LINES), many * LINES), many * LINES)
        spectra = []
        for which in range(2):
            high, low = spec_hi[which, rows, :], spec_lo[which, rows, :]
            spectra.append(
                dot(high, there_hi_ref[...])
                + (dot(low, there_hi_ref[...]) + dot(high, there_lo_ref[...]))
            )
        sig, ker = spectra
        sig_re, sig_im, ker_re, ker_im = sig[:, :COLS], sig[:, COLS:], ker[:, :COLS], ker[:, COLS:]
        product = jnp.concatenate(
            [sig_re * ker_re - sig_im * ker_im, sig_re * ker_im + sig_im * ker_re], axis=1
        )
        high, low = split(product)
        lines = dot(high, back_hi_ref[...]) + (
            dot(low, back_hi_ref[...]) + dot(high, back_lo_ref[...])
        )
        cos, sin = cos_ref[...], sin_ref[...]
        turned = []
        for k in range(many):
            re = lines[k * LINES : k * LINES + LINES, :COLS]
            im = lines[k * LINES : k * LINES + LINES, COLS:]
            turned.append(jnp.concatenate([re * cos - im * sin, im * cos + re * sin], axis=0))
        high, low = split(jnp.concatenate(turned, axis=1))
        values = dot(last_hi_ref[...], high) + (
            dot(last_hi_ref[...], low) + dot(last_lo_ref[...], high)
        )
        for k in range(many):
            result[pl.ds(step * many + k, LINES, stride=MINE), :] = values[
                :, k * COLS : k * COLS + COLS
            ]
        return carry

    lax.fori_loop(0, MINE // many, multiply, 0)
    for q in range(4):
        out_ref[:, :, q * 128 : q * 128 + 128] = (
            result[q * 512 : q * 512 + 512, :].reshape(SEQ, MINE, 128).astype(BF)
        )


def conv_call(received):
    consts = [jnp.asarray(t) for t in tables()]
    return pl.pallas_call(
        conv_kernel,
        out_shape=jax.ShapeDtypeStruct((SEQ, MINE, TOK), BF),
        scratch_shapes=[
            pltpu.VMEM((2, MINE * LINES, 128), F32),
            pltpu.VMEM((2, MINE * LINES, 2 * COLS), BF),
            pltpu.VMEM((2, MINE * LINES, 2 * COLS), BF),
            pltpu.VMEM((MINE * LINES, 128), F32),
        ],
        compiler_params=pltpu.CompilerParams(vmem_limit_bytes=40 * 2**20),
        cost_estimate=pl.CostEstimate(flops=5 * 10**9, bytes_accessed=2 * 2**20, transcendentals=0),
        name="conv",
    )(received, *consts)


def gate_kernel(conv_ref, gate_ref, key_ref, value_ref, skip_ref, out_ref):
    unit = eye(256)
    for half in range(2):
        rows = slice(half * 256, half * 256 + 256)
        conv = dot(unit, conv_ref[:, rows], ONES)
        signal = key_ref[rows, :].astype(F32) * value_ref[rows, :].astype(F32)
        gate = gate_ref[rows, :].astype(F32)
        out_ref[rows, :] = (gate * (conv + skip_ref[...] * signal)).astype(BF)


def gate_call(conv, gate, key, value, skip):
    return pl.pallas_call(
        gate_kernel,
        out_shape=jax.ShapeDtypeStruct((TOK, CH), BF),
        compiler_params=pltpu.CompilerParams(vmem_limit_bytes=32 * 2**20),
        cost_estimate=pl.CostEstimate(flops=2**28, bytes_accessed=5 * 2**19, transcendentals=0),
        name="gate",
    )(conv, gate, key, value, skip)


def pick_kernel(where_ref, query_ref, key_ref, value_ref, query_out, kv_out):
    core = where_ref[2]
    for k in range(4):
        cols = pl.ds(pl.multiple_of((2 * k + 1 - core) * HD, HD), HD)
        query_out[:, k * HD : k * HD + HD] = query_ref[:, cols]
    kv_out[:TOK, :] = key_ref[...]
    kv_out[TOK:, :] = value_ref[...]


def pick_call(where, query, keys, values):
    whole = pl.BlockSpec(memory_space=pltpu.VMEM)
    return pl.pallas_call(
        pick_kernel,
        out_shape=(
            jax.ShapeDtypeStruct((TOK, 4 * HD), BF),
            jax.ShapeDtypeStruct((2 * TOK, HD), BF),
        ),
        in_specs=[pl.BlockSpec(memory_space=pltpu.SMEM), whole, whole, whole],
        out_specs=(whole, whole),
        compiler_params=pltpu.CompilerParams(vmem_limit_bytes=16 * 2**20),
        cost_estimate=pl.CostEstimate(flops=0, bytes_accessed=2 * 2**20, transcendentals=0),
        name="pick",
    )(where, query, keys, values)


def attend_kernel(where_ref, query_ref, other_ref, *refs):
    own, behind = refs[0:4], refs[4:8]
    mine_out, other_out, mine_lse, other_lse = refs[8:]
    seq, line, core = where_ref[0], where_ref[1], where_ref[2]
    scale = HD**-0.5
    to_two = scale * math.log2(math.e)
    unit = eye(256)
    key_at = lax.broadcasted_iota(jnp.int32, (256, 256), 0)
    query_at = lax.broadcasted_iota(jnp.int32, (256, 256), 1)
    later = key_at > query_at
    for k in range(4):
        place = lax.rem(line + 4 - k, 4)
        value_t = jnp.concatenate(
            [behind[k][TOK:, :], own[k][TOK:, :]], axis=0
        ).T
        for member in range(2):
            if member == 0:
                cols = pl.ds(pl.multiple_of((2 * place + core) * HD, HD), HD)
                source, target, lse = query_ref, mine_out, mine_lse
            else:
                cols = pl.ds(pl.multiple_of(place * HD, HD), HD)
                source, target, lse = other_ref, other_out, other_lse
            out_cols = pl.ds(pl.multiple_of(place * HD, HD), HD)
            for half in range(2):
                rows = slice(half * 256, half * 256 + 256)
                query = source[rows, cols]
                back = dot(behind[k][:TOK, :], query, ONES)
                back = jnp.where(seq > 0, back, MASKED)
                tiles = [back]
                if half == 1:
                    tiles.append(dot(own[k][:256, :], query, ONES))
                last = dot(own[k][half * 256 : half * 256 + 256, :], query, ONES)
                tiles.append(jnp.where(later, MASKED, last))
                scores = jnp.concatenate(tiles, axis=0)
                peak = jnp.max(scores, axis=0, keepdims=True)
                expd = jnp.exp2(scores * to_two - peak * to_two)
                total = jnp.sum(expd, axis=0, keepdims=True)
                n_keys = scores.shape[0]
                mixed = dot(value_t[:, :n_keys], expd.astype(BF))
                normed = (mixed / total).astype(BF)
                target[rows, out_cols] = dot(unit, normed, ONES).astype(BF)
                lse[pl.ds(place, 1), rows] = peak * scale + jnp.log(total)


def attend_call(where, query, other, own, behind):
    whole = pl.BlockSpec(memory_space=pltpu.VMEM)
    return pl.pallas_call(
        attend_kernel,
        out_shape=(
            jax.ShapeDtypeStruct((TOK, 4 * HD), BF),
            jax.ShapeDtypeStruct((TOK, 4 * HD), BF),
            jax.ShapeDtypeStruct((4, TOK), F32),
            jax.ShapeDtypeStruct((4, TOK), F32),
        ),
        in_specs=[pl.BlockSpec(memory_space=pltpu.SMEM)] + [whole] * 10,
        out_specs=(whole,) * 4,
        compiler_params=pltpu.CompilerParams(vmem_limit_bytes=40 * 2**20),
        cost_estimate=pl.CostEstimate(
            flops=4 * 10**9, bytes_accessed=5 * 2**20, transcendentals=4 * 2**20
        ),
        name="attend",
    )(where, query, other, *own, *behind)


def merge_kernel(where_ref, mine_ref, got_ref, mine_lse, got_lse, out_ref, lse_ref):
    core = where_ref[2]
    for k in range(4):
        cols = slice(k * HD, k * HD + HD)
        at = pl.ds(pl.multiple_of((2 * k + core) * HD, HD), HD)
        out_ref[:, at] = mine_ref[:, cols]
        lse_ref[pl.ds(2 * k + core, 1), :] = mine_lse[k : k + 1, :]
        at = pl.ds(pl.multiple_of((2 * k + 1 - core) * HD, HD), HD)
        out_ref[:, at] = got_ref[:, cols]
        lse_ref[pl.ds(2 * k + 1 - core, 1), :] = got_lse[k : k + 1, :]


def merge_call(where, mine, got, mine_lse, got_lse):
    whole = pl.BlockSpec(memory_space=pltpu.VMEM)
    return pl.pallas_call(
        merge_kernel,
        out_shape=(
            jax.ShapeDtypeStruct((TOK, KVH * HD), BF),
            jax.ShapeDtypeStruct((KVH, TOK), F32),
        ),
        in_specs=[pl.BlockSpec(memory_space=pltpu.SMEM)] + [whole] * 4,
        out_specs=(whole, whole),
        compiler_params=pltpu.CompilerParams(vmem_limit_bytes=16 * 2**20),
        cost_estimate=pl.CostEstimate(flops=0, bytes_accessed=2 * 2**20, transcendentals=0),
        name="merge",
    )(where, mine, got, mine_lse, got_lse)


def to_line(x, chips):
    return lax.ppermute(x, "chan", [(c, (c + 2 * chips) % CHAN) for c in range(CHAN)])


def to_next(x, chips):
    pairs = [
        (s * CHAN + c, (s + 1) * CHAN + (c + 2 * chips) % CHAN)
        for s in range(SEQ - 1)
        for c in range(CHAN)
    ]
    return lax.ppermute(x, ("seq", "chan"), pairs)


def swap(x):
    return lax.ppermute(x, "chan", [(c, c ^ 1) for c in range(CHAN)])


def exchange(x):
    return lax.all_to_all(x, "seq", split_axis=0, concat_axis=0, tiled=True)


def local(
    hyena_gate, hyena_key, hyena_value, long_filter, skip_weight, attn_query, attn_keys, attn_values
):
    seq, chan = lax.axis_index("seq"), lax.axis_index("chan")
    where = jnp.stack([seq, chan // 2, chan % 2]).astype(jnp.int32)
    query = attn_query.reshape(TOK, KVH * HD)
    query_given, kv = pick_call(where, query, attn_keys, attn_values)
    own = [kv] + [to_line(kv, k) for k in (1, 2, 3)]
    behind = [to_next(kv, k) for k in (0, 1, 2, 3)]
    query_got = swap(query_given)
    turned = turn_call(hyena_key, hyena_value, long_filter)
    received = exchange(turned.reshape(2 * SEQ, MINE, TOK)).reshape(SEQ, 2, MINE, TOK)
    conv = conv_call(received)
    placed = exchange(conv)
    mine, given, mine_lse, given_lse = attend_call(where, query, query_got, own, behind)
    got, got_lse = swap(given), swap(given_lse)
    hyena_out = gate_call(
        placed.reshape(CH, TOK), hyena_gate, hyena_key, hyena_value, skip_weight.reshape(1, CH)
    )
    attn_out, attn_lse = merge_call(where, mine, got, mine_lse, got_lse)
    return (
        hyena_out,
        attn_out.reshape(TOK, 1, KVH * HD),
        attn_lse.reshape(1, KVH, TOK),
    )


def solution(mesh):
    return jax.shard_map(
        local,
        mesh=mesh,
        in_specs=(
            P("seq", "chan"),
            P("seq", "chan"),
            P("seq", "chan"),
            P("seq", "chan"),
            P("chan"),
            P("seq", "chan", None),
            P("seq", "chan"),
            P("seq", "chan"),
        ),
        out_specs=(P("seq", "chan"), P("seq", "chan", None), P("chan", None, "seq")),
        check_vma=False,
    )
```

```python
import functools
import math

import jax
import jax.numpy as jnp
import ml_dtypes
import numpy as np
from jax import lax
from jax.experimental import pallas as pl
from jax.experimental.pallas import tpu as pltpu
from jax.sharding import PartitionSpec as P

KVH = 8
HD = 128
TOK = 512
SEQ = 32
CHAN = 8
CH = 512
MINE = CH // SEQ
LINES = 128
COLS = 128
SIZE = 2 * LINES * COLS
BF = jnp.bfloat16
F32 = jnp.float32
MASKED = -1e30
ROOM = 58 * 2**20

ONES = (((1,), (1,)), ((), ()))
PLAIN = (((1,), (0,)), ((), ()))
FIRST = (((0,), (0,)), ((), ()))


def dot(a, b, dims=PLAIN):
    return lax.dot_general(a, b, dims, preferred_element_type=F32)


def split(x):
    high = x.astype(BF)
    return high, (x - high.astype(F32)).astype(BF)


def np_split(x):
    high = x.astype(ml_dtypes.bfloat16)
    low = (x - high.astype(np.float64)).astype(ml_dtypes.bfloat16)
    return high, low


def tables():
    rows = np.arange(LINES)
    line = 4 * (rows % SEQ) + rows // SEQ
    freq = np.arange(LINES) + 0.5
    angle = 2 * np.pi * np.outer(freq, line) / (2 * LINES)
    first = np.concatenate([np.cos(angle), -np.sin(angle)], axis=0)
    first_hi, first_lo = np_split(first)
    first_both = np.concatenate([first_hi, first_lo], axis=1)
    last_hi, last_lo = np_split(first.T * (2.0 / SIZE))
    turn = 2 * np.pi * np.outer(freq, np.arange(COLS)) / SIZE
    turn_cos, turn_sin = np.cos(turn).astype(np.float32), np.sin(turn).astype(np.float32)
    angle = 2 * np.pi * np.outer(np.arange(COLS), np.arange(COLS)) / COLS
    cos, sin = np.cos(angle), np.sin(angle)
    there = np.block([[cos, -sin], [sin, cos]])
    back = np.block([[cos, sin], [-sin, cos]])
    there_hi, there_lo = np_split(there)
    back_hi, back_lo = np_split(back)
    return (
        first_both,
        np.concatenate([last_hi, last_hi, last_lo], axis=1),
        turn_cos,
        turn_sin,
        np.concatenate([there_hi, there_hi, there_lo], axis=0),
        np.concatenate([back_hi, back_hi, back_lo], axis=0),
    )


def eye(n):
    at = lax.broadcasted_iota(jnp.int32, (n, n), 0) == lax.broadcasted_iota(jnp.int32, (n, n), 1)
    return at.astype(F32).astype(BF)


def turn_kernel(key_ref, value_ref, filter_ref, after_ref, out_ref):
    unit = eye(256)
    for half in range(2):
        cols = slice(half * 256, half * 256 + 256)
        groups = slice(half * 16, half * 16 + 16)
        signal = (key_ref[:, cols].astype(F32) * value_ref[:, cols].astype(F32)).astype(BF)
        out_ref[groups, 0] = dot(unit, signal, ONES).astype(BF).reshape(16, MINE, TOK)
        out_ref[groups, 1] = dot(unit, filter_ref[:, cols], ONES).astype(BF).reshape(16, MINE, TOK)


def turn_call(key, value, long_filter, after):
    whole = pl.BlockSpec(memory_space=pltpu.VMEM)
    return pl.pallas_call(
        turn_kernel,
        in_specs=[whole, whole, whole, pl.BlockSpec(memory_space=pl.ANY)],
        out_shape=jax.ShapeDtypeStruct((SEQ, 2, MINE, TOK), BF),
        compiler_params=pltpu.CompilerParams(vmem_limit_bytes=ROOM),
        cost_estimate=pl.CostEstimate(flops=2**29, bytes_accessed=5 * 2**19, transcendentals=0),
        name="turn",
    )(key, value, long_filter, after)


def conv_kernel(
    in_ref,
    first_ref,
    last_ref,
    cos_ref,
    sin_ref,
    there_ref,
    back_ref,
    out_ref,
    wide,
    spec,
    result,
):
    for which in range(2):
        for q in range(4):
            part = in_ref[:, which, :, q * 128 : q * 128 + 128].astype(F32)
            wide[which, q * 512 : q * 512 + 512, :] = part.reshape(512, 128)

    def spread(ch, carry):
        both = jnp.concatenate(
            [wide[which, pl.ds(ch, LINES, stride=MINE), :] for which in range(2)], axis=1
        ).astype(BF)
        both = jnp.concatenate([both, both], axis=0)
        lines = dot(first_ref[...], both)
        cos, sin = cos_ref[...], sin_ref[...]
        for which in range(2):
            re = lines[:LINES, which * COLS : which * COLS + COLS]
            im = lines[LINES:, which * COLS : which * COLS + COLS]
            turned = jnp.concatenate([re * cos + im * sin, im * cos - re * sin], axis=1)
            high, low = split(turned)
            rows = pl.ds(pl.multiple_of(ch * LINES, LINES), LINES)
            spec[which, rows, : 2 * COLS] = high
            spec[which, rows, 2 * COLS :] = low
        return carry

    lax.fori_loop(0, MINE, spread, 0, unroll=8)

    many = MINE

    def multiply(step, carry):
        rows = pl.ds(pl.multiple_of(step * (many * LINES), many * LINES), many * LINES)
        spectra = []
        for which in range(2):
            both = spec[which, rows, :]
            high = both[:, : 2 * COLS]
            spectra.append(dot(jnp.concatenate([both, high], axis=1), there_ref[...]))
        sig, ker = spectra
        sig_re, sig_im, ker_re, ker_im = sig[:, :COLS], sig[:, COLS:], ker[:, :COLS], ker[:, COLS:]
        product = jnp.concatenate(
            [sig_re * ker_re - sig_im * ker_im, sig_re * ker_im + sig_im * ker_re], axis=1
        )
        high, low = split(product)
        lines = dot(jnp.concatenate([high, low, high], axis=1), back_ref[...])
        cos, sin = cos_ref[...], sin_ref[...]
        turned = []
        for k in range(many):
            re = lines[k * LINES : k * LINES + LINES, :COLS]
            im = lines[k * LINES : k * LINES + LINES, COLS:]
            turned.append(jnp.concatenate([re * cos - im * sin, im * cos + re * sin], axis=0))
        high, low = split(jnp.concatenate(turned, axis=1))
        values = dot(last_ref[...], jnp.concatenate([high, low, high], axis=0))
        for k in range(many):
            result[pl.ds(step * many + k, LINES, stride=MINE), :] = values[
                :, k * COLS : k * COLS + COLS
            ]
        return carry

    lax.fori_loop(0, MINE // many, multiply, 0)
    for q in range(4):
        out_ref[:, :, q * 128 : q * 128 + 128] = (
            result[q * 512 : q * 512 + 512, :].reshape(SEQ, MINE, 128).astype(BF)
        )


def conv_call(received):
    consts = [jnp.asarray(t) for t in tables()]
    return pl.pallas_call(
        conv_kernel,
        out_shape=jax.ShapeDtypeStruct((SEQ, MINE, TOK), BF),
        scratch_shapes=[
            pltpu.VMEM((2, MINE * LINES, 128), F32),
            pltpu.VMEM((2, MINE * LINES, 4 * COLS), BF),
            pltpu.VMEM((MINE * LINES, 128), F32),
        ],
        compiler_params=pltpu.CompilerParams(vmem_limit_bytes=58 * 2**20),
        cost_estimate=pl.CostEstimate(flops=5 * 10**9, bytes_accessed=2 * 2**20, transcendentals=0),
        name="conv",
    )(received, *consts)


def gate_kernel(conv_ref, gate_ref, key_ref, value_ref, skip_ref, out_ref):
    unit = eye(256)
    for half in range(2):
        rows = slice(half * 256, half * 256 + 256)
        conv = dot(unit, conv_ref[:, rows], ONES)
        signal = key_ref[rows, :].astype(F32) * value_ref[rows, :].astype(F32)
        gate = gate_ref[rows, :].astype(F32)
        out_ref[rows, :] = (gate * (conv + skip_ref[...] * signal)).astype(BF)


def gate_call(conv, gate, key, value, skip):
    return pl.pallas_call(
        gate_kernel,
        out_shape=jax.ShapeDtypeStruct((TOK, CH), BF),
        compiler_params=pltpu.CompilerParams(vmem_limit_bytes=14 * 2**20),
        cost_estimate=pl.CostEstimate(flops=2**28, bytes_accessed=5 * 2**19, transcendentals=0),
        name="gate",
    )(conv, gate, key, value, skip)


def pack_kernel(key_ref, value_ref, out_ref):
    out_ref[:TOK, :] = key_ref[...]
    out_ref[TOK:, :] = value_ref[...]


def pack_call(keys, values):
    return pl.pallas_call(
        pack_kernel,
        out_shape=jax.ShapeDtypeStruct((2 * TOK, HD), BF),
        compiler_params=pltpu.CompilerParams(vmem_limit_bytes=ROOM),
        cost_estimate=pl.CostEstimate(flops=0, bytes_accessed=2**19, transcendentals=0),
        name="pack",
    )(keys, values)


SCALE = HD**-0.5
TO_TWO = SCALE * math.log2(math.e)
TILE = 256
HALVES = TOK // TILE


def pipelined(jobs, first, second):
    ahead = first(jobs[0])
    for i, job in enumerate(jobs):
        now = ahead
        if i + 1 < len(jobs):
            ahead = first(jobs[i + 1])
        second(job, now)


def tile_rows(h):
    return slice(h * TILE, h * TILE + TILE)


def own_kernel(where_ref, query_ref, other_ref, *refs):
    pieces = refs[0:4]
    mine_acc, other_acc, peak_ref, total_ref, keys = refs[4:]
    line, core = where_ref[1], where_ref[2]
    for k in range(4):
        keys[lax.rem(line + 4 - k, 4), :, :HD] = pieces[k][...]
        keys[k, TOK:, HD:] = jnp.ones((TOK, HD), BF)
    at_query = lax.broadcasted_iota(jnp.int32, (TILE, TILE), 0)
    at_key = lax.broadcasted_iota(jnp.int32, (TILE, TILE), 1)
    later = at_key > at_query
    lane = lax.broadcasted_iota(jnp.int32, (TILE, HD), 1)
    peaks = [jnp.zeros((TILE, HD), F32) for _ in range(HALVES)]
    totals = [jnp.zeros((TILE, HD), F32) for _ in range(HALVES)]

    def score(job):
        place, member, h = job
        cols = pl.ds(pl.multiple_of((2 * place + core) * HD, HD), HD)
        query = (query_ref, other_ref)[member][tile_rows(h), cols]
        here = dot(query, keys[place, : (h + 1) * TILE, :HD], ONES)
        last = jnp.where(later, MASKED, here[:, h * TILE :])
        return jnp.concatenate([here[:, : h * TILE], last], axis=1) if h else last

    def finish(job, scores):
        place, member, h = job
        peak = jnp.max(scores, axis=1, keepdims=True)
        weights = jnp.exp2(scores * TO_TWO - peak * TO_TWO).astype(BF)
        mixed = dot(weights, keys[place, TOK : TOK + (h + 1) * TILE, :])
        (mine_acc, other_acc)[member][place, tile_rows(h), :] = mixed[:, :HD]
        at = lane == member * 4 + place
        peaks[h] = jnp.where(at, peak, peaks[h])
        totals[h] = jnp.where(at, mixed[:, HD:], totals[h])

    jobs = [(p, m, h) for p in range(4) for m in range(2) for h in range(HALVES)]
    pipelined(jobs, score, finish)
    for h in range(HALVES):
        peak_ref[tile_rows(h), :] = peaks[h]
        total_ref[tile_rows(h), :] = totals[h]


def own_call(where, query, other, pieces):
    whole = pl.BlockSpec(memory_space=pltpu.VMEM)
    acc = jax.ShapeDtypeStruct((4, TOK, HD), F32)
    stat = jax.ShapeDtypeStruct((TOK, HD), F32)
    return pl.pallas_call(
        own_kernel,
        out_shape=(acc, acc, stat, stat),
        in_specs=[pl.BlockSpec(memory_space=pltpu.SMEM)] + [whole] * 6,
        out_specs=(whole,) * 4,
        scratch_shapes=[pltpu.VMEM((4, 2 * TOK, 2 * HD), BF)],
        compiler_params=pltpu.CompilerParams(vmem_limit_bytes=14 * 2**20),
        cost_estimate=pl.CostEstimate(
            flops=4 * 10**10, bytes_accessed=4 * 2**20, transcendentals=2 * 2**20
        ),
        name="own",
    )(where, query, other, *pieces)


def back_kernel(member, where_ref, query_ref, *refs):
    pieces = refs[0:4]
    acc_ref, peak_ref, total_ref, out_ref, lse_ref, keys = refs[4:]
    seq, line, core = where_ref[0], where_ref[1], where_ref[2]
    crossed = lax.rem(seq, 4) == 0
    for k in range(4):
        place = lax.rem(line + 4 - k, 4)
        keys[jnp.where(crossed, 3 - place, place), :, :HD] = pieces[k][...]
        keys[k, TOK:, HD:] = jnp.ones((TOK, HD), BF)
    lane = lax.broadcasted_iota(jnp.int32, (TILE, HD), 1)
    lses = [jnp.zeros((TILE, HD), F32) for _ in range(HALVES)]

    def score(job):
        place, h = job
        cols = pl.ds(pl.multiple_of((2 * place + core) * HD, HD), HD)
        scores = dot(query_ref[tile_rows(h), cols], keys[place, :TOK, :HD], ONES)
        return jnp.where(seq > 0, scores, MASKED)

    def finish(job, scores):
        place, h = job
        column = member * 4 + place
        own_peak = peak_ref[tile_rows(h), column : column + 1]
        own_total = total_ref[tile_rows(h), column : column + 1]
        peak = jnp.maximum(jnp.max(scores, axis=1, keepdims=True), own_peak)
        weights = jnp.exp2(scores * TO_TWO - peak * TO_TWO).astype(BF)
        mixed = dot(weights, keys[place, TOK:, :])
        keep = jnp.exp2((own_peak - peak) * TO_TWO)
        total = mixed[:, HD:] + keep * own_total
        out = (mixed[:, :HD] + keep * acc_ref[place, tile_rows(h), :]) / total
        out_ref[tile_rows(h), place * HD : place * HD + HD] = out.astype(BF)
        lses[h] = jnp.where(lane == place, peak * SCALE + jnp.log(total), lses[h])

    pipelined([(p, h) for p in range(4) for h in range(HALVES)], score, finish)
    for h in range(HALVES):
        lse_ref[:, tile_rows(h)] = lses[h].T[:4]


def back_call(member, where, query, pieces, acc, peak, total):
    whole = pl.BlockSpec(memory_space=pltpu.VMEM)

    def kernel(*refs):
        back_kernel(member, *refs)

    return pl.pallas_call(
        kernel,
        out_shape=(
            jax.ShapeDtypeStruct((TOK, 4 * HD), BF),
            jax.ShapeDtypeStruct((4, TOK), F32),
        ),
        in_specs=[pl.BlockSpec(memory_space=pltpu.SMEM)] + [whole] * 8,
        out_specs=(whole,) * 2,
        scratch_shapes=[pltpu.VMEM((4, 2 * TOK, 2 * HD), BF)],
        compiler_params=pltpu.CompilerParams(vmem_limit_bytes=14 * 2**20),
        cost_estimate=pl.CostEstimate(
            flops=10**11, bytes_accessed=4 * 2**20, transcendentals=2 * 2**20
        ),
        name="back",
    )(where, query, *pieces, acc, peak, total)


def merge_kernel(where_ref, mine_ref, got_ref, mine_lse, got_lse, out_ref, lse_ref):
    core = where_ref[2]
    for k in range(4):
        cols = slice(k * HD, k * HD + HD)
        at = pl.ds(pl.multiple_of((2 * k + core) * HD, HD), HD)
        out_ref[:, at] = mine_ref[:, cols]
        lse_ref[pl.ds(2 * k + core, 1), :] = mine_lse[k : k + 1, :]
        at = pl.ds(pl.multiple_of((2 * k + 1 - core) * HD, HD), HD)
        out_ref[:, at] = got_ref[:, cols]
        lse_ref[pl.ds(2 * k + 1 - core, 1), :] = got_lse[k : k + 1, :]


def merge_call(where, mine, got, mine_lse, got_lse):
    whole = pl.BlockSpec(memory_space=pltpu.VMEM)
    return pl.pallas_call(
        merge_kernel,
        out_shape=(
            jax.ShapeDtypeStruct((TOK, KVH * HD), BF),
            jax.ShapeDtypeStruct((KVH, TOK), F32),
        ),
        in_specs=[pl.BlockSpec(memory_space=pltpu.SMEM)] + [whole] * 4,
        out_specs=(whole, whole),
        compiler_params=pltpu.CompilerParams(vmem_limit_bytes=14 * 2**20),
        cost_estimate=pl.CostEstimate(flops=0, bytes_accessed=2 * 2**20, transcendentals=0),
        name="merge",
    )(where, mine, got, mine_lse, got_lse)


def to_line(x, chips):
    return lax.ppermute(x, "chan", [(c, (c + 2 * chips) % CHAN) for c in range(CHAN)])


def to_next(x):
    pairs = [
        (s * CHAN + c, (s + 1) * CHAN + (c if s % 4 != 3 else 2 * (3 - c // 2) + c % 2))
        for s in range(SEQ - 1)
        for c in range(CHAN)
    ]
    return lax.ppermute(x, ("seq", "chan"), pairs)


def swap(x):
    return lax.ppermute(x, "chan", [(c, c ^ 1) for c in range(CHAN)])


def exchange(x):
    return lax.all_to_all(x, "seq", split_axis=0, concat_axis=0, tiled=True)


def local(
    hyena_gate, hyena_key, hyena_value, long_filter, skip_weight, attn_query, attn_keys, attn_values
):
    seq, chan = lax.axis_index("seq"), lax.axis_index("chan")
    where = jnp.stack([seq, chan // 2, chan % 2]).astype(jnp.int32)
    query = attn_query.reshape(TOK, KVH * HD)
    kv = pack_call(attn_keys, attn_values)
    query_got = swap(query)
    kv_behind = to_next(kv)
    own = [kv] + [to_line(kv, k) for k in (1, 2, 3)]
    turned = turn_call(hyena_key, hyena_value, long_filter, kv)
    received = exchange(turned.reshape(2 * SEQ, MINE, TOK)).reshape(SEQ, 2, MINE, TOK)
    mine_acc, given_acc, peak, total = own_call(where, query, query_got, own)
    received, kv_behind, peak = lax.optimization_barrier((received, kv_behind, peak))
    behind = [kv_behind] + [to_line(kv_behind, k) for k in (1, 2, 3)]
    conv = conv_call(received)
    placed = exchange(conv)
    given, given_lse = back_call(1, where, query_got, behind, given_acc, peak, total)
    got, got_lse = swap(given), swap(given_lse)
    mine, mine_lse = back_call(0, where, query, behind, mine_acc, peak, total)
    hyena_out = gate_call(
        placed.reshape(CH, TOK), hyena_gate, hyena_key, hyena_value, skip_weight.reshape(1, CH)
    )
    attn_out, attn_lse = merge_call(where, mine, got, mine_lse, got_lse)
    return (
        hyena_out,
        attn_out.reshape(TOK, 1, KVH * HD),
        attn_lse.reshape(1, KVH, TOK),
    )


def solution(mesh):
    return jax.shard_map(
        local,
        mesh=mesh,
        in_specs=(
            P("seq", "chan"),
            P("seq", "chan"),
            P("seq", "chan"),
            P("seq", "chan"),
            P("chan"),
            P("seq", "chan", None),
            P("seq", "chan"),
            P("seq", "chan"),
        ),
        out_specs=(P("seq", "chan"), P("seq", "chan", None), P("chan", None, "seq")),
        check_vma=False,
    )
```

```python
import functools
import math

import jax
import jax.numpy as jnp
import ml_dtypes
import numpy as np
from jax import lax
from jax.experimental import pallas as pl
from jax.experimental.pallas import tpu as pltpu
from jax.sharding import PartitionSpec as P

KVH = 8
HD = 128
TOK = 512
SEQ = 32
CHAN = 8
CH = 512
MINE = CH // SEQ
LINES = 128
COLS = 128
SIZE = 2 * LINES * COLS
BF = jnp.bfloat16
F32 = jnp.float32
MASKED = -1e30
ROOM = 58 * 2**20

ONES = (((1,), (1,)), ((), ()))
PLAIN = (((1,), (0,)), ((), ()))
FIRST = (((0,), (0,)), ((), ()))


def dot(a, b, dims=PLAIN):
    return lax.dot_general(a, b, dims, preferred_element_type=F32)


def split(x):
    high = x.astype(BF)
    return high, (x - high.astype(F32)).astype(BF)


def np_split(x):
    high = x.astype(ml_dtypes.bfloat16)
    low = (x - high.astype(np.float64)).astype(ml_dtypes.bfloat16)
    return high, low


def tables():
    rows = np.arange(LINES)
    line = 4 * (rows % SEQ) + rows // SEQ
    freq = np.arange(LINES) + 0.5
    angle = 2 * np.pi * np.outer(freq, line) / (2 * LINES)
    first = np.concatenate([np.cos(angle), -np.sin(angle)], axis=0)
    first_hi, first_lo = np_split(first)
    first_both = np.concatenate([first_hi, first_lo], axis=1)
    last_hi, last_lo = np_split(first.T * (2.0 / SIZE))
    turn = 2 * np.pi * np.outer(freq, np.arange(COLS)) / SIZE
    turn_cos, turn_sin = np.cos(turn).astype(np.float32), np.sin(turn).astype(np.float32)
    angle = 2 * np.pi * np.outer(np.arange(COLS), np.arange(COLS)) / COLS
    cos, sin = np.cos(angle), np.sin(angle)
    there = np.block([[cos, -sin], [sin, cos]])
    back = np.block([[cos, sin], [-sin, cos]])
    there_hi, there_lo = np_split(there)
    back_hi, back_lo = np_split(back)
    factors = [first_both, there_hi, there_hi, there_lo, back_hi, back_hi, back_lo]
    factors += [last_hi, last_hi, last_lo]
    return np.concatenate(factors, axis=0), np.concatenate([turn_cos, turn_sin], axis=1)


def eye(n):
    at = lax.broadcasted_iota(jnp.int32, (n, n), 0) == lax.broadcasted_iota(jnp.int32, (n, n), 1)
    return at.astype(F32).astype(BF)


def turn_kernel(key_ref, value_ref, filter_ref, after_ref, out_ref):
    unit = eye(256)
    for half in range(2):
        cols = slice(half * 256, half * 256 + 256)
        groups = slice(half * 16, half * 16 + 16)
        signal = (key_ref[:, cols].astype(F32) * value_ref[:, cols].astype(F32)).astype(BF)
        out_ref[groups, 0] = dot(unit, signal, ONES).astype(BF).reshape(16, MINE, TOK)
        out_ref[groups, 1] = dot(unit, filter_ref[:, cols], ONES).astype(BF).reshape(16, MINE, TOK)


def turn_call(key, value, long_filter, after):
    whole = pl.BlockSpec(memory_space=pltpu.VMEM)
    return pl.pallas_call(
        turn_kernel,
        in_specs=[whole, whole, whole, pl.BlockSpec(memory_space=pl.ANY)],
        out_shape=jax.ShapeDtypeStruct((SEQ, 2, MINE, TOK), BF),
        compiler_params=pltpu.CompilerParams(vmem_limit_bytes=ROOM),
        cost_estimate=pl.CostEstimate(flops=2**29, bytes_accessed=5 * 2**19, transcendentals=0),
        name="turn",
    )(key, value, long_filter, after)


def conv_kernel(
    in_ref,
    factor_ref,
    turn_ref,
    out_ref,
    wide,
    spec,
    result,
):
    def factor(start, size):
        return factor_ref[start : start + size, :]

    cos, sin = turn_ref[:, :COLS], turn_ref[:, COLS:]
    for which in range(2):
        for q in range(4):
            part = in_ref[:, which, :, q * 128 : q * 128 + 128].astype(F32)
            wide[which, q * 512 : q * 512 + 512, :] = part.reshape(512, 128)

    def spread(ch, carry):
        both = jnp.concatenate(
            [wide[which, pl.ds(ch, LINES, stride=MINE), :] for which in range(2)], axis=1
        ).astype(BF)
        both = jnp.concatenate([both, both], axis=0)
        lines = dot(factor(0, 256), both)
        for which in range(2):
            re = lines[:LINES, which * COLS : which * COLS + COLS]
            im = lines[LINES:, which * COLS : which * COLS + COLS]
            turned = jnp.concatenate([re * cos + im * sin, im * cos - re * sin], axis=1)
            high, low = split(turned)
            rows = pl.ds(pl.multiple_of(ch * LINES, LINES), LINES)
            spec[which, rows, : 2 * COLS] = high
            spec[which, rows, 2 * COLS :] = low
        return carry

    lax.fori_loop(0, MINE, spread, 0, unroll=8)

    many = MINE

    def multiply(step, carry):
        rows = pl.ds(pl.multiple_of(step * (many * LINES), many * LINES), many * LINES)
        spectra = []
        for which in range(2):
            both = spec[which, rows, :]
            high = both[:, : 2 * COLS]
            spectra.append(dot(jnp.concatenate([both, high], axis=1), factor(256, 768)))
        sig, ker = spectra
        sig_re, sig_im, ker_re, ker_im = sig[:, :COLS], sig[:, COLS:], ker[:, :COLS], ker[:, COLS:]
        product = jnp.concatenate(
            [sig_re * ker_re - sig_im * ker_im, sig_re * ker_im + sig_im * ker_re], axis=1
        )
        high, low = split(product)
        lines = dot(jnp.concatenate([high, low, high], axis=1), factor(1024, 768))
        turned = []
        for k in range(many):
            re = lines[k * LINES : k * LINES + LINES, :COLS]
            im = lines[k * LINES : k * LINES + LINES, COLS:]
            turned.append(jnp.concatenate([re * cos - im * sin, im * cos + re * sin], axis=0))
        high, low = split(jnp.concatenate(turned, axis=1))
        last = jnp.concatenate([factor(1792 + LINES * i, LINES) for i in range(3)], axis=1)
        values = dot(last, jnp.concatenate([high, low, high], axis=0))
        for k in range(many):
            result[pl.ds(step * many + k, LINES, stride=MINE), :] = values[
                :, k * COLS : k * COLS + COLS
            ]
        return carry

    lax.fori_loop(0, MINE // many, multiply, 0)
    for q in range(4):
        out_ref[:, :, q * 128 : q * 128 + 128] = (
            result[q * 512 : q * 512 + 512, :].reshape(SEQ, MINE, 128).astype(BF)
        )


def conv_call(received):
    consts = [jnp.asarray(t) for t in tables()]
    return pl.pallas_call(
        conv_kernel,
        out_shape=jax.ShapeDtypeStruct((SEQ, MINE, TOK), BF),
        scratch_shapes=[
            pltpu.VMEM((2, MINE * LINES, 128), F32),
            pltpu.VMEM((2, MINE * LINES, 4 * COLS), BF),
            pltpu.VMEM((MINE * LINES, 128), F32),
        ],
        compiler_params=pltpu.CompilerParams(vmem_limit_bytes=58 * 2**20),
        cost_estimate=pl.CostEstimate(flops=5 * 10**9, bytes_accessed=2 * 2**20, transcendentals=0),
        name="conv",
    )(received, *consts)


def gate_kernel(conv_ref, gate_ref, key_ref, value_ref, skip_ref, out_ref):
    unit = eye(256)
    for half in range(2):
        rows = slice(half * 256, half * 256 + 256)
        conv = dot(unit, conv_ref[:, rows], ONES)
        signal = key_ref[rows, :].astype(F32) * value_ref[rows, :].astype(F32)
        gate = gate_ref[rows, :].astype(F32)
        out_ref[rows, :] = (gate * (conv + skip_ref[...] * signal)).astype(BF)


def gate_call(conv, gate, key, value, skip):
    return pl.pallas_call(
        gate_kernel,
        out_shape=jax.ShapeDtypeStruct((TOK, CH), BF),
        compiler_params=pltpu.CompilerParams(vmem_limit_bytes=14 * 2**20),
        cost_estimate=pl.CostEstimate(flops=2**28, bytes_accessed=5 * 2**19, transcendentals=0),
        name="gate",
    )(conv, gate, key, value, skip)


def pack_kernel(key_ref, value_ref, out_ref):
    out_ref[:TOK, :] = key_ref[...]
    out_ref[TOK:, :] = value_ref[...]


def pack_call(keys, values):
    return pl.pallas_call(
        pack_kernel,
        out_shape=jax.ShapeDtypeStruct((2 * TOK, HD), BF),
        compiler_params=pltpu.CompilerParams(vmem_limit_bytes=ROOM),
        cost_estimate=pl.CostEstimate(flops=0, bytes_accessed=2**19, transcendentals=0),
        name="pack",
    )(keys, values)


SCALE = HD**-0.5
TO_TWO = SCALE * math.log2(math.e)
TILE = 256
HALVES = TOK // TILE


def pipelined(jobs, first, second):
    ahead = first(jobs[0])
    for i, job in enumerate(jobs):
        now = ahead
        if i + 1 < len(jobs):
            ahead = first(jobs[i + 1])
        second(job, now)


def tile_rows(h):
    return slice(h * TILE, h * TILE + TILE)


def lay_out(keys, pieces, line):
    kept, below, above, across, far = pieces
    keys[line, :, :HD] = kept[...]
    keys[lax.rem(line + 2, 4), :, :HD] = across[...]
    keys[lax.rem(line + 3, 4), :, :HD] = jnp.where(line > 0, below[...], far[...])
    keys[lax.rem(line + 1, 4), :, :HD] = jnp.where(line < 3, above[...], far[...])
    for k in range(4):
        keys[k, TOK:, HD:] = jnp.ones((TOK, HD), BF)


def own_kernel(where_ref, query_ref, other_ref, *refs):
    pieces = refs[0:5]
    mine_acc, other_acc, peak_ref, total_ref, keys = refs[5:]
    line, core = where_ref[1], where_ref[2]
    lay_out(keys, pieces, line)
    at_query = lax.broadcasted_iota(jnp.int32, (TILE, TILE), 0)
    at_key = lax.broadcasted_iota(jnp.int32, (TILE, TILE), 1)
    later = at_key > at_query
    lane = lax.broadcasted_iota(jnp.int32, (TILE, HD), 1)
    peaks = [jnp.zeros((TILE, HD), F32) for _ in range(HALVES)]
    totals = [jnp.zeros((TILE, HD), F32) for _ in range(HALVES)]

    def score(job):
        place, member, h = job
        cols = pl.ds(pl.multiple_of((2 * place + core) * HD, HD), HD)
        query = (query_ref, other_ref)[member][tile_rows(h), cols]
        here = dot(query, keys[place, : (h + 1) * TILE, :HD], ONES)
        last = jnp.where(later, MASKED, here[:, h * TILE :])
        return jnp.concatenate([here[:, : h * TILE], last], axis=1) if h else last

    def finish(job, scores):
        place, member, h = job
        peak = jnp.max(scores, axis=1, keepdims=True)
        weights = jnp.exp2(scores * TO_TWO - peak * TO_TWO).astype(BF)
        mixed = dot(weights, keys[place, TOK : TOK + (h + 1) * TILE, :])
        (mine_acc, other_acc)[member][place, tile_rows(h), :] = mixed[:, :HD]
        at = lane == member * 4 + place
        peaks[h] = jnp.where(at, peak, peaks[h])
        totals[h] = jnp.where(at, mixed[:, HD:], totals[h])

    jobs = [(p, m, h) for p in range(4) for m in range(2) for h in range(HALVES)]
    pipelined(jobs, score, finish)
    for h in range(HALVES):
        peak_ref[tile_rows(h), :] = peaks[h]
        total_ref[tile_rows(h), :] = totals[h]


def own_call(where, query, other, pieces):
    whole = pl.BlockSpec(memory_space=pltpu.VMEM)
    acc = jax.ShapeDtypeStruct((4, TOK, HD), F32)
    stat = jax.ShapeDtypeStruct((TOK, HD), F32)
    return pl.pallas_call(
        own_kernel,
        out_shape=(acc, acc, stat, stat),
        in_specs=[pl.BlockSpec(memory_space=pltpu.SMEM)] + [whole] * 7,
        out_specs=(whole,) * 4,
        scratch_shapes=[pltpu.VMEM((4, 2 * TOK, 2 * HD), BF)],
        compiler_params=pltpu.CompilerParams(vmem_limit_bytes=14 * 2**20),
        cost_estimate=pl.CostEstimate(
            flops=4 * 10**10, bytes_accessed=4 * 2**20, transcendentals=2 * 2**20
        ),
        name="own",
    )(where, query, other, *pieces)


def back_kernel(member, where_ref, query_ref, *refs):
    pieces = refs[0:4]
    acc_ref, peak_ref, total_ref, out_ref, lse_ref, keys = refs[4:]
    seq, line, core = where_ref[0], where_ref[1], where_ref[2]
    crossed = lax.rem(seq, 4) == 0
    for k in range(4):
        place = lax.rem(line + 4 - k, 4)
        keys[jnp.where(crossed, 3 - place, place), :, :HD] = pieces[k][...]
        keys[k, TOK:, HD:] = jnp.ones((TOK, HD), BF)
    lane = lax.broadcasted_iota(jnp.int32, (TILE, HD), 1)
    lses = [jnp.zeros((TILE, HD), F32) for _ in range(HALVES)]

    def score(job):
        place, h = job
        cols = pl.ds(pl.multiple_of((2 * place + core) * HD, HD), HD)
        scores = dot(query_ref[tile_rows(h), cols], keys[place, :TOK, :HD], ONES)
        return jnp.where(seq > 0, scores, MASKED)

    def finish(job, scores):
        place, h = job
        column = member * 4 + place
        own_peak = peak_ref[tile_rows(h), column : column + 1]
        own_total = total_ref[tile_rows(h), column : column + 1]
        peak = jnp.maximum(jnp.max(scores, axis=1, keepdims=True), own_peak)
        weights = jnp.exp2(scores * TO_TWO - peak * TO_TWO).astype(BF)
        mixed = dot(weights, keys[place, TOK:, :])
        keep = jnp.exp2((own_peak - peak) * TO_TWO)
        total = mixed[:, HD:] + keep * own_total
        out = (mixed[:, :HD] + keep * acc_ref[place, tile_rows(h), :]) / total
        out_ref[tile_rows(h), place * HD : place * HD + HD] = out.astype(BF)
        lses[h] = jnp.where(lane == place, peak * SCALE + jnp.log(total), lses[h])

    pipelined([(p, h) for p in range(4) for h in range(HALVES)], score, finish)
    for h in range(HALVES):
        lse_ref[:, tile_rows(h)] = lses[h].T[:4]


def back_call(member, where, query, pieces, acc, peak, total):
    whole = pl.BlockSpec(memory_space=pltpu.VMEM)

    def kernel(*refs):
        back_kernel(member, *refs)

    return pl.pallas_call(
        kernel,
        out_shape=(
            jax.ShapeDtypeStruct((TOK, 4 * HD), BF),
            jax.ShapeDtypeStruct((4, TOK), F32),
        ),
        in_specs=[pl.BlockSpec(memory_space=pltpu.SMEM)] + [whole] * 8,
        out_specs=(whole,) * 2,
        scratch_shapes=[pltpu.VMEM((4, 2 * TOK, 2 * HD), BF)],
        compiler_params=pltpu.CompilerParams(vmem_limit_bytes=14 * 2**20),
        cost_estimate=pl.CostEstimate(
            flops=10**11, bytes_accessed=4 * 2**20, transcendentals=2 * 2**20
        ),
        name="back",
    )(where, query, *pieces, acc, peak, total)


def merge_kernel(where_ref, mine_ref, got_ref, mine_lse, got_lse, out_ref, lse_ref):
    core = where_ref[2]
    for k in range(4):
        cols = slice(k * HD, k * HD + HD)
        at = pl.ds(pl.multiple_of((2 * k + core) * HD, HD), HD)
        out_ref[:, at] = mine_ref[:, cols]
        lse_ref[pl.ds(2 * k + core, 1), :] = mine_lse[k : k + 1, :]
        at = pl.ds(pl.multiple_of((2 * k + 1 - core) * HD, HD), HD)
        out_ref[:, at] = got_ref[:, cols]
        lse_ref[pl.ds(2 * k + 1 - core, 1), :] = got_lse[k : k + 1, :]


def merge_call(where, mine, got, mine_lse, got_lse):
    whole = pl.BlockSpec(memory_space=pltpu.VMEM)
    return pl.pallas_call(
        merge_kernel,
        out_shape=(
            jax.ShapeDtypeStruct((TOK, KVH * HD), BF),
            jax.ShapeDtypeStruct((KVH, TOK), F32),
        ),
        in_specs=[pl.BlockSpec(memory_space=pltpu.SMEM)] + [whole] * 4,
        out_specs=(whole, whole),
        compiler_params=pltpu.CompilerParams(vmem_limit_bytes=14 * 2**20),
        cost_estimate=pl.CostEstimate(flops=0, bytes_accessed=2 * 2**20, transcendentals=0),
        name="merge",
    )(where, mine, got, mine_lse, got_lse)


def one_line(x, moves):
    pairs = [(2 * i + core, 2 * j + core) for i, j in moves for core in range(2)]
    return lax.ppermute(x, "chan", pairs)


def gather_near(x):
    below = one_line(x, [(0, 1), (1, 2), (2, 3)])
    above = one_line(x, [(1, 0), (2, 1), (3, 2)])
    across = one_line(x, [(0, 2), (1, 3), (2, 0), (3, 1)])
    return [x, below, above, across]


def around(x, chips):
    return one_line(x, [(i, (i + chips) % 4) for i in range(4)])


def gather_far(across):
    return one_line(across, [(2, 3), (1, 0)])


def to_next(x):
    pairs = [
        (s * CHAN + c, (s + 1) * CHAN + (c if s % 4 != 3 else 2 * (3 - c // 2) + c % 2))
        for s in range(SEQ - 1)
        for c in range(CHAN)
    ]
    return lax.ppermute(x, ("seq", "chan"), pairs)


def swap(x):
    return lax.ppermute(x, "chan", [(c, c ^ 1) for c in range(CHAN)])


def exchange(x):
    return lax.all_to_all(x, "seq", split_axis=0, concat_axis=0, tiled=True)


def local(
    hyena_gate, hyena_key, hyena_value, long_filter, skip_weight, attn_query, attn_keys, attn_values
):
    seq, chan = lax.axis_index("seq"), lax.axis_index("chan")
    where = jnp.stack([seq, chan // 2, chan % 2]).astype(jnp.int32)
    query = attn_query.reshape(TOK, KVH * HD)
    kv = pack_call(attn_keys, attn_values)
    query_got = swap(query)
    kv_behind = to_next(kv)
    own = gather_near(kv)
    turned = turn_call(hyena_key, hyena_value, long_filter, kv)
    across, _, kv_behind = lax.optimization_barrier((own[3], turned, kv_behind))
    own.append(gather_far(across))
    received = exchange(turned.reshape(2 * SEQ, MINE, TOK)).reshape(SEQ, 2, MINE, TOK)
    mine_acc, given_acc, peak, total = own_call(where, query, query_got, own)
    kv_behind, peak = lax.optimization_barrier((kv_behind, peak))
    behind = [kv_behind] + [around(kv_behind, k) for k in (1, 2, 3)]
    received, peak = lax.optimization_barrier((received, peak))
    conv = conv_call(received)
    placed = exchange(conv)
    given, given_lse = back_call(1, where, query_got, behind, given_acc, peak, total)
    got, got_lse = swap(given), swap(given_lse)
    mine, mine_lse = back_call(0, where, query, behind, mine_acc, peak, total)
    hyena_out = gate_call(
        placed.reshape(CH, TOK), hyena_gate, hyena_key, hyena_value, skip_weight.reshape(1, CH)
    )
    attn_out, attn_lse = merge_call(where, mine, got, mine_lse, got_lse)
    return (
        hyena_out,
        attn_out.reshape(TOK, 1, KVH * HD),
        attn_lse.reshape(1, KVH, TOK),
    )


def solution(mesh):
    return jax.shard_map(
        local,
        mesh=mesh,
        in_specs=(
            P("seq", "chan"),
            P("seq", "chan"),
            P("seq", "chan"),
            P("seq", "chan"),
            P("chan"),
            P("seq", "chan", None),
            P("seq", "chan"),
            P("seq", "chan"),
        ),
        out_specs=(P("seq", "chan"), P("seq", "chan", None), P("chan", None, "seq")),
        check_vma=False,
    )
```

```python
import functools
import math

import jax
import jax.numpy as jnp
import ml_dtypes
import numpy as np
from jax import lax
from jax.experimental import pallas as pl
from jax.experimental.pallas import tpu as pltpu
from jax.sharding import PartitionSpec as P

KVH = 8
HD = 128
TOK = 512
SEQ = 32
CHAN = 8
CH = 512
MINE = CH // SEQ
LINES = 128
COLS = 128
SIZE = 2 * LINES * COLS
BF = jnp.bfloat16
F32 = jnp.float32
MASKED = -1e30
ROOM = 58 * 2**20

ONES = (((1,), (1,)), ((), ()))
PLAIN = (((1,), (0,)), ((), ()))
FIRST = (((0,), (0,)), ((), ()))


def dot(a, b, dims=PLAIN):
    return lax.dot_general(a, b, dims, preferred_element_type=F32)


def split(x):
    high = x.astype(BF)
    return high, (x - high.astype(F32)).astype(BF)


def np_split(x):
    high = x.astype(ml_dtypes.bfloat16)
    low = (x - high.astype(np.float64)).astype(ml_dtypes.bfloat16)
    return high, low


def tables():
    rows = np.arange(LINES)
    line = 4 * (rows % SEQ) + rows // SEQ
    freq = np.arange(LINES) + 0.5
    angle = 2 * np.pi * np.outer(freq, line) / (2 * LINES)
    first = np.concatenate([np.cos(angle), -np.sin(angle)], axis=0)
    first_hi, first_lo = np_split(first)
    first_both = np.concatenate([first_hi, first_lo], axis=1)
    last_hi, last_lo = np_split(first.T * (2.0 / SIZE))
    turn = 2 * np.pi * np.outer(freq, np.arange(COLS)) / SIZE
    turn_cos, turn_sin = np.cos(turn).astype(np.float32), np.sin(turn).astype(np.float32)
    angle = 2 * np.pi * np.outer(np.arange(COLS), np.arange(COLS)) / COLS
    cos, sin = np.cos(angle), np.sin(angle)
    there = np.block([[cos, -sin], [sin, cos]])
    back = np.block([[cos, sin], [-sin, cos]])
    there_hi, there_lo = np_split(there)
    back_hi, back_lo = np_split(back)
    factors = [first_both, there_hi, there_lo, back_hi, back_lo, last_hi, last_lo]
    return np.concatenate(factors, axis=0), np.concatenate([turn_cos, turn_sin], axis=1)


def eye(n):
    at = lax.broadcasted_iota(jnp.int32, (n, n), 0) == lax.broadcasted_iota(jnp.int32, (n, n), 1)
    return at.astype(F32).astype(BF)


def turn_kernel(key_ref, value_ref, filter_ref, after_ref, out_ref):
    unit = eye(256)
    for half in range(2):
        cols = slice(half * 256, half * 256 + 256)
        groups = slice(half * 16, half * 16 + 16)
        signal = (key_ref[:, cols].astype(F32) * value_ref[:, cols].astype(F32)).astype(BF)
        out_ref[groups, 0] = dot(unit, signal, ONES).astype(BF).reshape(16, MINE, TOK)
        out_ref[groups, 1] = dot(unit, filter_ref[:, cols], ONES).astype(BF).reshape(16, MINE, TOK)


def turn_call(key, value, long_filter, after):
    whole = pl.BlockSpec(memory_space=pltpu.VMEM)
    return pl.pallas_call(
        turn_kernel,
        in_specs=[whole, whole, whole, pl.BlockSpec(memory_space=pl.ANY)],
        out_shape=jax.ShapeDtypeStruct((SEQ, 2, MINE, TOK), BF),
        compiler_params=pltpu.CompilerParams(vmem_limit_bytes=ROOM),
        cost_estimate=pl.CostEstimate(flops=2**29, bytes_accessed=5 * 2**19, transcendentals=0),
        name="turn",
    )(key, value, long_filter, after)


def conv_kernel(
    in_ref,
    factor_ref,
    turn_ref,
    out_ref,
    wide,
    spec,
    result,
):
    def factor(start, size):
        return factor_ref[start : start + size, :]

    def three(start, size, axis):
        high, low = factor(start, size), factor(start + size, size)
        return jnp.concatenate([high, high, low], axis=axis)

    cos, sin = turn_ref[:, :COLS], turn_ref[:, COLS:]
    for which in range(2):
        for q in range(4):
            part = in_ref[:, which, :, q * 128 : q * 128 + 128].astype(F32)
            wide[which, q * 512 : q * 512 + 512, :] = part.reshape(512, 128)

    def spread(ch, carry):
        both = jnp.concatenate(
            [wide[which, pl.ds(ch, LINES, stride=MINE), :] for which in range(2)], axis=1
        ).astype(BF)
        both = jnp.concatenate([both, both], axis=0)
        lines = dot(factor(0, 256), both)
        for which in range(2):
            re = lines[:LINES, which * COLS : which * COLS + COLS]
            im = lines[LINES:, which * COLS : which * COLS + COLS]
            turned = jnp.concatenate([re * cos + im * sin, im * cos - re * sin], axis=1)
            high, low = split(turned)
            rows = pl.ds(pl.multiple_of(ch * LINES, LINES), LINES)
            spec[which, rows, : 2 * COLS] = high
            spec[which, rows, 2 * COLS :] = low
        return carry

    lax.fori_loop(0, MINE, spread, 0, unroll=8)

    many = MINE

    def multiply(step, carry):
        rows = pl.ds(pl.multiple_of(step * (many * LINES), many * LINES), many * LINES)
        spectra = []
        for which in range(2):
            both = spec[which, rows, :]
            high = both[:, : 2 * COLS]
            spectra.append(dot(jnp.concatenate([both, high], axis=1), three(256, 256, 0)))
        sig, ker = spectra
        sig_re, sig_im, ker_re, ker_im = sig[:, :COLS], sig[:, COLS:], ker[:, :COLS], ker[:, COLS:]
        product = jnp.concatenate(
            [sig_re * ker_re - sig_im * ker_im, sig_re * ker_im + sig_im * ker_re], axis=1
        )
        high, low = split(product)
        lines = dot(jnp.concatenate([high, low, high], axis=1), three(768, 256, 0))
        turned = []
        for k in range(many):
            re = lines[k * LINES : k * LINES + LINES, :COLS]
            im = lines[k * LINES : k * LINES + LINES, COLS:]
            turned.append(jnp.concatenate([re * cos - im * sin, im * cos + re * sin], axis=0))
        high, low = split(jnp.concatenate(turned, axis=1))
        values = dot(three(1280, LINES, 1), jnp.concatenate([high, low, high], axis=0))
        for k in range(many):
            result[pl.ds(step * many + k, LINES, stride=MINE), :] = values[
                :, k * COLS : k * COLS + COLS
            ]
        return carry

    lax.fori_loop(0, MINE // many, multiply, 0)
    for q in range(4):
        out_ref[:, :, q * 128 : q * 128 + 128] = (
            result[q * 512 : q * 512 + 512, :].reshape(SEQ, MINE, 128).astype(BF)
        )


def conv_call(received):
    consts = [jnp.asarray(t) for t in tables()]
    return pl.pallas_call(
        conv_kernel,
        out_shape=jax.ShapeDtypeStruct((SEQ, MINE, TOK), BF),
        scratch_shapes=[
            pltpu.VMEM((2, MINE * LINES, 128), F32),
            pltpu.VMEM((2, MINE * LINES, 4 * COLS), BF),
            pltpu.VMEM((MINE * LINES, 128), F32),
        ],
        compiler_params=pltpu.CompilerParams(vmem_limit_bytes=58 * 2**20),
        cost_estimate=pl.CostEstimate(flops=5 * 10**9, bytes_accessed=2 * 2**20, transcendentals=0),
        name="conv",
    )(received, *consts)


def gate_kernel(conv_ref, gate_ref, key_ref, value_ref, skip_ref, out_ref):
    conv = dot(eye(256), conv_ref[...], ONES)
    signal = key_ref[...].astype(F32) * value_ref[...].astype(F32)
    gate = gate_ref[...].astype(F32)
    out_ref[...] = (gate * (conv + skip_ref[...] * signal)).astype(BF)


def gate_call(conv, gate, key, value, skip):
    rows = pl.BlockSpec((256, CH), lambda i: (i, 0))
    return pl.pallas_call(
        gate_kernel,
        grid=(2,),
        in_specs=[
            pl.BlockSpec((CH, 256), lambda i: (0, i)),
            rows,
            rows,
            rows,
            pl.BlockSpec((1, CH), lambda i: (0, 0)),
        ],
        out_specs=rows,
        out_shape=jax.ShapeDtypeStruct((TOK, CH), BF),
        compiler_params=pltpu.CompilerParams(vmem_limit_bytes=ROOM),
        cost_estimate=pl.CostEstimate(flops=2**28, bytes_accessed=5 * 2**19, transcendentals=0),
        name="gate",
    )(conv, gate, key, value, skip)


def pack_kernel(key_ref, value_ref, out_ref):
    out_ref[:TOK, :] = key_ref[...]
    out_ref[TOK:, :] = value_ref[...]


def pack_call(keys, values):
    return pl.pallas_call(
        pack_kernel,
        out_shape=jax.ShapeDtypeStruct((2 * TOK, HD), BF),
        compiler_params=pltpu.CompilerParams(vmem_limit_bytes=ROOM),
        cost_estimate=pl.CostEstimate(flops=0, bytes_accessed=2**19, transcendentals=0),
        name="pack",
    )(keys, values)


SCALE = HD**-0.5
TO_TWO = SCALE * math.log2(math.e)
TILE = 256
HALVES = TOK // TILE


def pipelined(jobs, first, second):
    ahead = first(jobs[0])
    for i, job in enumerate(jobs):
        now = ahead
        if i + 1 < len(jobs):
            ahead = first(jobs[i + 1])
        second(job, now)


def tile_rows(h):
    return slice(h * TILE, h * TILE + TILE)


def lay_out(keys, pieces, line):
    kept, below, above, across, far = pieces
    keys[line, :, :HD] = kept[...]
    keys[lax.rem(line + 2, 4), :, :HD] = across[...]
    keys[lax.rem(line + 3, 4), :, :HD] = jnp.where(line > 0, below[...], far[...])
    keys[lax.rem(line + 1, 4), :, :HD] = jnp.where(line < 3, above[...], far[...])
    for k in range(4):
        keys[k, TOK:, HD:] = jnp.ones((TOK, HD), BF)


def own_kernel(where_ref, query_ref, other_ref, *refs):
    pieces = refs[0:5]
    mine_acc, other_acc, peak_ref, total_ref, keys = refs[5:]
    line, core = where_ref[1], where_ref[2]
    lay_out(keys, pieces, line)
    at_query = lax.broadcasted_iota(jnp.int32, (TILE, TILE), 0)
    at_key = lax.broadcasted_iota(jnp.int32, (TILE, TILE), 1)
    later = at_key > at_query
    lane = lax.broadcasted_iota(jnp.int32, (TILE, HD), 1)
    peaks = [jnp.zeros((TILE, HD), F32) for _ in range(HALVES)]
    totals = [jnp.zeros((TILE, HD), F32) for _ in range(HALVES)]

    def score(job):
        place, member, h = job
        cols = pl.ds(pl.multiple_of((2 * place + core) * HD, HD), HD)
        query = (query_ref, other_ref)[member][tile_rows(h), cols]
        here = dot(query, keys[place, : (h + 1) * TILE, :HD], ONES)
        last = jnp.where(later, MASKED, here[:, h * TILE :])
        return jnp.concatenate([here[:, : h * TILE], last], axis=1) if h else last

    def finish(job, scores):
        place, member, h = job
        peak = jnp.max(scores, axis=1, keepdims=True)
        weights = jnp.exp2(scores * TO_TWO - peak * TO_TWO).astype(BF)
        mixed = dot(weights, keys[place, TOK : TOK + (h + 1) * TILE, :])
        (mine_acc, other_acc)[member][place, tile_rows(h), :] = mixed[:, :HD]
        at = lane == member * 4 + place
        peaks[h] = jnp.where(at, peak, peaks[h])
        totals[h] = jnp.where(at, mixed[:, HD:], totals[h])

    jobs = [(p, m, h) for p in range(4) for m in range(2) for h in range(HALVES)]
    pipelined(jobs, score, finish)
    for h in range(HALVES):
        peak_ref[tile_rows(h), :] = peaks[h]
        total_ref[tile_rows(h), :] = totals[h]


def own_call(where, query, other, pieces):
    whole = pl.BlockSpec(memory_space=pltpu.VMEM)
    acc = jax.ShapeDtypeStruct((4, TOK, HD), F32)
    stat = jax.ShapeDtypeStruct((TOK, HD), F32)
    return pl.pallas_call(
        own_kernel,
        out_shape=(acc, acc, stat, stat),
        in_specs=[pl.BlockSpec(memory_space=pltpu.SMEM)] + [whole] * 7,
        out_specs=(whole,) * 4,
        scratch_shapes=[pltpu.VMEM((4, 2 * TOK, 2 * HD), BF)],
        compiler_params=pltpu.CompilerParams(vmem_limit_bytes=14 * 2**20),
        cost_estimate=pl.CostEstimate(
            flops=4 * 10**10, bytes_accessed=4 * 2**20, transcendentals=2 * 2**20
        ),
        name="own",
    )(where, query, other, *pieces)


def back_kernel(member, where_ref, query_ref, *refs):
    pieces = refs[0:4]
    acc_in, peak_ref, total_ref, out_ref, lse_ref, keys, acc_ref, sem = refs[4:]
    copy = pltpu.make_async_copy(acc_in, acc_ref, sem)
    copy.start()
    seq, line, core = where_ref[0], where_ref[1], where_ref[2]
    crossed = lax.rem(seq, 4) == 0
    for k in range(4):
        place = lax.rem(line + 4 - k, 4)
        keys[jnp.where(crossed, 3 - place, place), :, :HD] = pieces[k][...]
        keys[k, TOK:, HD:] = jnp.ones((TOK, HD), BF)
    lane = lax.broadcasted_iota(jnp.int32, (TILE, HD), 1)
    lses = [jnp.zeros((TILE, HD), F32) for _ in range(HALVES)]

    def score(job):
        place, h = job
        cols = pl.ds(pl.multiple_of((2 * place + core) * HD, HD), HD)
        scores = dot(query_ref[tile_rows(h), cols], keys[place, :TOK, :HD], ONES)
        return jnp.where(seq > 0, scores, MASKED)

    def finish(job, scores):
        place, h = job
        if job == (0, 0):
            copy.wait()
        column = member * 4 + place
        own_peak = peak_ref[tile_rows(h), column : column + 1]
        own_total = total_ref[tile_rows(h), column : column + 1]
        peak = jnp.maximum(jnp.max(scores, axis=1, keepdims=True), own_peak)
        weights = jnp.exp2(scores * TO_TWO - peak * TO_TWO).astype(BF)
        mixed = dot(weights, keys[place, TOK:, :])
        keep = jnp.exp2((own_peak - peak) * TO_TWO)
        total = mixed[:, HD:] + keep * own_total
        out = (mixed[:, :HD] + keep * acc_ref[place, tile_rows(h), :]) / total
        out_ref[tile_rows(h), place * HD : place * HD + HD] = out.astype(BF)
        lses[h] = jnp.where(lane == place, peak * SCALE + jnp.log(total), lses[h])

    pipelined([(p, h) for p in range(4) for h in range(HALVES)], score, finish)
    for h in range(HALVES):
        lse_ref[:, tile_rows(h)] = lses[h].T[:4]


def back_call(member, where, query, pieces, acc, peak, total):
    whole = pl.BlockSpec(memory_space=pltpu.VMEM)

    def kernel(*refs):
        back_kernel(member, *refs)

    return pl.pallas_call(
        kernel,
        out_shape=(
            jax.ShapeDtypeStruct((TOK, 4 * HD), BF),
            jax.ShapeDtypeStruct((4, TOK), F32),
        ),
        in_specs=[pl.BlockSpec(memory_space=pltpu.SMEM)] + [whole] * 5
        + [pl.BlockSpec(memory_space=pl.ANY), whole, whole],
        out_specs=(whole,) * 2,
        scratch_shapes=[
            pltpu.VMEM((4, 2 * TOK, 2 * HD), BF),
            pltpu.VMEM((4, TOK, HD), F32),
            pltpu.SemaphoreType.DMA,
        ],
        compiler_params=pltpu.CompilerParams(vmem_limit_bytes=14 * 2**20),
        cost_estimate=pl.CostEstimate(
            flops=10**11, bytes_accessed=4 * 2**20, transcendentals=2 * 2**20
        ),
        name="back",
    )(where, query, *pieces, acc, peak, total)


def merge_kernel(where_ref, mine_ref, got_ref, mine_lse, got_lse, out_ref, lse_ref):
    core = where_ref[2]
    for k in range(4):
        cols = slice(k * HD, k * HD + HD)
        at = pl.ds(pl.multiple_of((2 * k + core) * HD, HD), HD)
        out_ref[:, at] = mine_ref[:, cols]
        lse_ref[pl.ds(2 * k + core, 1), :] = mine_lse[k : k + 1, :]
        at = pl.ds(pl.multiple_of((2 * k + 1 - core) * HD, HD), HD)
        out_ref[:, at] = got_ref[:, cols]
        lse_ref[pl.ds(2 * k + 1 - core, 1), :] = got_lse[k : k + 1, :]


def merge_call(where, mine, got, mine_lse, got_lse):
    whole = pl.BlockSpec(memory_space=pltpu.VMEM)
    return pl.pallas_call(
        merge_kernel,
        out_shape=(
            jax.ShapeDtypeStruct((TOK, KVH * HD), BF),
            jax.ShapeDtypeStruct((KVH, TOK), F32),
        ),
        in_specs=[pl.BlockSpec(memory_space=pltpu.SMEM)] + [whole] * 4,
        out_specs=(whole, whole),
        compiler_params=pltpu.CompilerParams(vmem_limit_bytes=14 * 2**20),
        cost_estimate=pl.CostEstimate(flops=0, bytes_accessed=2 * 2**20, transcendentals=0),
        name="merge",
    )(where, mine, got, mine_lse, got_lse)


def one_line(x, moves):
    pairs = [(2 * i + core, 2 * j + core) for i, j in moves for core in range(2)]
    return lax.ppermute(x, "chan", pairs)


def gather_near(x):
    below = one_line(x, [(0, 1), (1, 2), (2, 3)])
    above = one_line(x, [(1, 0), (2, 1), (3, 2)])
    across = one_line(x, [(0, 2), (1, 3), (2, 0), (3, 1)])
    return [x, below, above, across]


def around(x, chips):
    return one_line(x, [(i, (i + chips) % 4) for i in range(4)])


def gather_far(across):
    return one_line(across, [(2, 3), (1, 0)])


def to_next(x):
    pairs = [
        (s * CHAN + c, (s + 1) * CHAN + (c if s % 4 != 3 else 2 * (3 - c // 2) + c % 2))
        for s in range(SEQ - 1)
        for c in range(CHAN)
    ]
    return lax.ppermute(x, ("seq", "chan"), pairs)


def swap(x):
    return lax.ppermute(x, "chan", [(c, c ^ 1) for c in range(CHAN)])


def exchange(x):
    return lax.all_to_all(x, "seq", split_axis=0, concat_axis=0, tiled=True)


def local(
    hyena_gate, hyena_key, hyena_value, long_filter, skip_weight, attn_query, attn_keys, attn_values
):
    seq, chan = lax.axis_index("seq"), lax.axis_index("chan")
    where = jnp.stack([seq, chan // 2, chan % 2]).astype(jnp.int32)
    query = attn_query.reshape(TOK, KVH * HD)
    kv = pack_call(attn_keys, attn_values)
    query_got = swap(query)
    kv_behind = to_next(kv)
    own = gather_near(kv)
    turned = turn_call(hyena_key, hyena_value, long_filter, kv)
    across, _, kv_behind = lax.optimization_barrier((own[3], turned, kv_behind))
    own.append(gather_far(across))
    received = exchange(turned.reshape(2 * SEQ, MINE, TOK)).reshape(SEQ, 2, MINE, TOK)
    mine_acc, given_acc, peak, total = own_call(where, query, query_got, own)
    kv_behind, peak = lax.optimization_barrier((kv_behind, peak))
    behind = [kv_behind] + [around(kv_behind, k) for k in (1, 2, 3)]
    received, peak = lax.optimization_barrier((received, peak))
    conv = conv_call(received)
    placed = exchange(conv)
    given, given_lse = back_call(1, where, query_got, behind, given_acc, peak, total)
    got, got_lse = swap(given), swap(given_lse)
    mine, mine_lse = back_call(0, where, query, behind, mine_acc, peak, total)
    hyena_out = gate_call(
        placed.reshape(CH, TOK), hyena_gate, hyena_key, hyena_value, skip_weight.reshape(1, CH)
    )
    attn_out, attn_lse = merge_call(where, mine, got, mine_lse, got_lse)
    return (
        hyena_out,
        attn_out.reshape(TOK, 1, KVH * HD),
        attn_lse.reshape(1, KVH, TOK),
    )


def solution(mesh):
    return jax.shard_map(
        local,
        mesh=mesh,
        in_specs=(
            P("seq", "chan"),
            P("seq", "chan"),
            P("seq", "chan"),
            P("seq", "chan"),
            P("chan"),
            P("seq", "chan", None),
            P("seq", "chan"),
            P("seq", "chan"),
        ),
        out_specs=(P("seq", "chan"), P("seq", "chan", None), P("chan", None, "seq")),
        check_vma=False,
    )
```

```python
import functools
import math

import jax
import jax.numpy as jnp
import ml_dtypes
import numpy as np
from jax import lax
from jax.experimental import pallas as pl
from jax.experimental.pallas import tpu as pltpu
from jax.sharding import PartitionSpec as P

KVH = 8
HD = 128
TOK = 512
SEQ = 32
CHAN = 8
CH = 512
MINE = CH // SEQ
LINES = 128
COLS = 128
SIZE = 2 * LINES * COLS
BF = jnp.bfloat16
F32 = jnp.float32
MASKED = -1e30
ROOM = 58 * 2**20

ONES = (((1,), (1,)), ((), ()))
PLAIN = (((1,), (0,)), ((), ()))
FIRST = (((0,), (0,)), ((), ()))


def dot(a, b, dims=PLAIN):
    return lax.dot_general(a, b, dims, preferred_element_type=F32)


def split(x):
    high = x.astype(BF)
    return high, (x - high.astype(F32)).astype(BF)


def np_split(x):
    high = x.astype(ml_dtypes.bfloat16)
    low = (x - high.astype(np.float64)).astype(ml_dtypes.bfloat16)
    return high, low


def tables():
    rows = np.arange(LINES)
    line = 4 * (rows % SEQ) + rows // SEQ
    freq = np.arange(LINES) + 0.5
    angle = 2 * np.pi * np.outer(freq, line) / (2 * LINES)
    first = np.concatenate([np.cos(angle), -np.sin(angle)], axis=0)
    first_hi, first_lo = np_split(first)
    first_both = np.concatenate([first_hi, first_lo], axis=1)
    last_hi, last_lo = np_split(first.T * (2.0 / SIZE))
    turn = 2 * np.pi * np.outer(freq, np.arange(COLS)) / SIZE
    turn_cos, turn_sin = np.cos(turn).astype(np.float32), np.sin(turn).astype(np.float32)
    angle = 2 * np.pi * np.outer(np.arange(COLS), np.arange(COLS)) / COLS
    cos, sin = np.cos(angle), np.sin(angle)
    there = np.block([[cos, -sin], [sin, cos]])
    back = np.block([[cos, sin], [-sin, cos]])
    there_hi, there_lo = np_split(there)
    back_hi, back_lo = np_split(back)
    factors = [first_both, there_hi, there_lo, back_hi, back_lo, last_hi, last_lo]
    return np.concatenate(factors, axis=0), np.concatenate([turn_cos, turn_sin], axis=1)


def eye(n):
    at = lax.broadcasted_iota(jnp.int32, (n, n), 0) == lax.broadcasted_iota(jnp.int32, (n, n), 1)
    return at.astype(F32).astype(BF)


def turn_kernel(key_ref, value_ref, filter_ref, after_ref, out_ref):
    unit = eye(256)
    for half in range(2):
        cols = slice(half * 256, half * 256 + 256)
        groups = slice(half * 16, half * 16 + 16)
        signal = (key_ref[:, cols].astype(F32) * value_ref[:, cols].astype(F32)).astype(BF)
        out_ref[groups, 0] = dot(unit, signal, ONES).astype(BF).reshape(16, MINE, TOK)
        out_ref[groups, 1] = dot(unit, filter_ref[:, cols], ONES).astype(BF).reshape(16, MINE, TOK)


def turn_call(key, value, long_filter, after):
    whole = pl.BlockSpec(memory_space=pltpu.VMEM)
    return pl.pallas_call(
        turn_kernel,
        in_specs=[whole, whole, whole, pl.BlockSpec(memory_space=pl.ANY)],
        out_shape=jax.ShapeDtypeStruct((SEQ, 2, MINE, TOK), BF),
        compiler_params=pltpu.CompilerParams(vmem_limit_bytes=ROOM),
        cost_estimate=pl.CostEstimate(flops=2**29, bytes_accessed=5 * 2**19, transcendentals=0),
        name="turn",
    )(key, value, long_filter, after)


def conv_kernel(
    in_ref,
    factor_ref,
    turn_ref,
    out_ref,
    wide,
    spec,
    result,
):
    def factor(start, size):
        return factor_ref[start : start + size, :]

    def three(start, size, axis):
        high, low = factor(start, size), factor(start + size, size)
        return jnp.concatenate([high, high, low], axis=axis)

    cos, sin = turn_ref[:, :COLS], turn_ref[:, COLS:]
    for which in range(2):
        for q in range(4):
            part = in_ref[:, which, :, q * 128 : q * 128 + 128].astype(F32)
            wide[which, q * 512 : q * 512 + 512, :] = part.reshape(512, 128)

    def spread(ch, carry):
        both = jnp.concatenate(
            [wide[which, pl.ds(ch, LINES, stride=MINE), :] for which in range(2)], axis=1
        ).astype(BF)
        both = jnp.concatenate([both, both], axis=0)
        lines = dot(factor(0, 256), both)
        for which in range(2):
            re = lines[:LINES, which * COLS : which * COLS + COLS]
            im = lines[LINES:, which * COLS : which * COLS + COLS]
            turned = jnp.concatenate([re * cos + im * sin, im * cos - re * sin], axis=1)
            high, low = split(turned)
            rows = pl.ds(pl.multiple_of(ch * LINES, LINES), LINES)
            spec[which, rows, : 2 * COLS] = high
            spec[which, rows, 2 * COLS :] = low
        return carry

    lax.fori_loop(0, MINE, spread, 0, unroll=8)

    many = MINE

    def multiply(step, carry):
        rows = pl.ds(pl.multiple_of(step * (many * LINES), many * LINES), many * LINES)
        spectra = []
        for which in range(2):
            both = spec[which, rows, :]
            high = both[:, : 2 * COLS]
            spectra.append(dot(jnp.concatenate([both, high], axis=1), three(256, 256, 0)))
        sig, ker = spectra
        sig_re, sig_im, ker_re, ker_im = sig[:, :COLS], sig[:, COLS:], ker[:, :COLS], ker[:, COLS:]
        product = jnp.concatenate(
            [sig_re * ker_re - sig_im * ker_im, sig_re * ker_im + sig_im * ker_re], axis=1
        )
        high, low = split(product)
        lines = dot(jnp.concatenate([high, low, high], axis=1), three(768, 256, 0))
        turned = []
        for k in range(many):
            re = lines[k * LINES : k * LINES + LINES, :COLS]
            im = lines[k * LINES : k * LINES + LINES, COLS:]
            turned.append(jnp.concatenate([re * cos - im * sin, im * cos + re * sin], axis=0))
        high, low = split(jnp.concatenate(turned, axis=1))
        values = dot(three(1280, LINES, 1), jnp.concatenate([high, low, high], axis=0))
        for k in range(many):
            result[pl.ds(step * many + k, LINES, stride=MINE), :] = values[
                :, k * COLS : k * COLS + COLS
            ]
        return carry

    lax.fori_loop(0, MINE // many, multiply, 0)
    for q in range(4):
        out_ref[:, :, q * 128 : q * 128 + 128] = (
            result[q * 512 : q * 512 + 512, :].reshape(SEQ, MINE, 128).astype(BF)
        )


def conv_call(received):
    consts = [jnp.asarray(t) for t in tables()]
    return pl.pallas_call(
        conv_kernel,
        out_shape=jax.ShapeDtypeStruct((SEQ, MINE, TOK), BF),
        scratch_shapes=[
            pltpu.VMEM((2, MINE * LINES, 128), F32),
            pltpu.VMEM((2, MINE * LINES, 4 * COLS), BF),
            pltpu.VMEM((MINE * LINES, 128), F32),
        ],
        compiler_params=pltpu.CompilerParams(vmem_limit_bytes=58 * 2**20),
        cost_estimate=pl.CostEstimate(flops=5 * 10**9, bytes_accessed=2 * 2**20, transcendentals=0),
        name="conv",
    )(received, *consts)


def gate_kernel(conv_ref, gate_ref, key_ref, value_ref, skip_ref, out_ref):
    conv = dot(eye(256), conv_ref[...], ONES)
    signal = key_ref[...].astype(F32) * value_ref[...].astype(F32)
    gate = gate_ref[...].astype(F32)
    out_ref[...] = (gate * (conv + skip_ref[...] * signal)).astype(BF)


def gate_call(conv, gate, key, value, skip):
    rows = pl.BlockSpec((256, CH), lambda i: (i, 0))
    return pl.pallas_call(
        gate_kernel,
        grid=(2,),
        in_specs=[
            pl.BlockSpec((CH, 256), lambda i: (0, i)),
            rows,
            rows,
            rows,
            pl.BlockSpec((1, CH), lambda i: (0, 0)),
        ],
        out_specs=rows,
        out_shape=jax.ShapeDtypeStruct((TOK, CH), BF),
        compiler_params=pltpu.CompilerParams(vmem_limit_bytes=ROOM),
        cost_estimate=pl.CostEstimate(flops=2**28, bytes_accessed=5 * 2**19, transcendentals=0),
        name="gate",
    )(conv, gate, key, value, skip)


def pack_kernel(key_ref, value_ref, out_ref):
    out_ref[:TOK, :] = key_ref[...]
    out_ref[TOK:, :] = value_ref[...]


def pack_call(keys, values):
    return pl.pallas_call(
        pack_kernel,
        out_shape=jax.ShapeDtypeStruct((2 * TOK, HD), BF),
        compiler_params=pltpu.CompilerParams(vmem_limit_bytes=ROOM),
        cost_estimate=pl.CostEstimate(flops=0, bytes_accessed=2**19, transcendentals=0),
        name="pack",
    )(keys, values)


SCALE = HD**-0.5
TO_TWO = SCALE * math.log2(math.e)
TILE = 256
HALVES = TOK // TILE


def pipelined(jobs, first, second):
    ahead = first(jobs[0])
    for i, job in enumerate(jobs):
        now = ahead
        if i + 1 < len(jobs):
            ahead = first(jobs[i + 1])
        second(job, now)


def tile_rows(h):
    return slice(h * TILE, h * TILE + TILE)


def lay_out(keys, pieces, line):
    kept, below, above, across, far = pieces
    keys[line, :, :HD] = kept[...]
    keys[lax.rem(line + 2, 4), :, :HD] = across[...]
    keys[lax.rem(line + 3, 4), :, :HD] = jnp.where(line > 0, below[...], far[...])
    keys[lax.rem(line + 1, 4), :, :HD] = jnp.where(line < 3, above[...], far[...])
    for k in range(4):
        keys[k, TOK:, HD:] = jnp.ones((TOK, HD), BF)


def own_kernel(where_ref, query_ref, other_ref, *refs):
    pieces = refs[0:5]
    mine_acc, other_acc, peak_ref, total_ref, keys = refs[5:]
    line, core = where_ref[1], where_ref[2]
    lay_out(keys, pieces, line)
    at_query = lax.broadcasted_iota(jnp.int32, (TILE, TILE), 0)
    at_key = lax.broadcasted_iota(jnp.int32, (TILE, TILE), 1)
    later = at_key > at_query
    lane = lax.broadcasted_iota(jnp.int32, (TILE, HD), 1)
    peaks = [jnp.zeros((TILE, HD), F32) for _ in range(HALVES)]
    totals = [jnp.zeros((TILE, HD), F32) for _ in range(HALVES)]

    def score(job):
        place, member, h = job
        cols = pl.ds(pl.multiple_of((2 * place + core) * HD, HD), HD)
        query = (query_ref, other_ref)[member][tile_rows(h), cols]
        here = dot(query, keys[place, : (h + 1) * TILE, :HD], ONES)
        last = jnp.where(later, MASKED, here[:, h * TILE :])
        return jnp.concatenate([here[:, : h * TILE], last], axis=1) if h else last

    def finish(job, scores):
        place, member, h = job
        peak = jnp.max(scores, axis=1, keepdims=True)
        weights = jnp.exp2(scores * TO_TWO - peak * TO_TWO).astype(BF)
        mixed = dot(weights, keys[place, TOK : TOK + (h + 1) * TILE, :])
        (mine_acc, other_acc)[member][place, tile_rows(h), :] = mixed[:, :HD]
        at = lane == member * 4 + place
        peaks[h] = jnp.where(at, peak, peaks[h])
        totals[h] = jnp.where(at, mixed[:, HD:], totals[h])

    jobs = [(p, m, h) for p in range(4) for m in range(2) for h in range(HALVES)]
    pipelined(jobs, score, finish)
    for h in range(HALVES):
        peak_ref[tile_rows(h), :] = peaks[h]
        total_ref[tile_rows(h), :] = totals[h]


def own_call(where, query, other, pieces):
    whole = pl.BlockSpec(memory_space=pltpu.VMEM)
    acc = jax.ShapeDtypeStruct((4, TOK, HD), F32)
    stat = jax.ShapeDtypeStruct((TOK, HD), F32)
    return pl.pallas_call(
        own_kernel,
        out_shape=(acc, acc, stat, stat),
        in_specs=[pl.BlockSpec(memory_space=pltpu.SMEM)] + [whole] * 7,
        out_specs=(whole,) * 4,
        scratch_shapes=[pltpu.VMEM((4, 2 * TOK, 2 * HD), BF)],
        compiler_params=pltpu.CompilerParams(vmem_limit_bytes=14 * 2**20),
        cost_estimate=pl.CostEstimate(
            flops=4 * 10**10, bytes_accessed=4 * 2**20, transcendentals=2 * 2**20
        ),
        name="own",
    )(where, query, other, *pieces)


def back_kernel(member, where_ref, query_ref, *refs):
    pieces = refs[0:4]
    acc_in, peak_ref, total_ref, out_ref, lse_ref, keys, acc_ref, sem = refs[4:]
    copy = pltpu.make_async_copy(acc_in, acc_ref, sem)
    copy.start()
    seq, line, core = where_ref[0], where_ref[1], where_ref[2]
    crossed = lax.rem(seq, 4) == 0
    for k in range(4):
        place = lax.rem(line + 4 - k, 4)
        keys[jnp.where(crossed, 3 - place, place), :, :HD] = pieces[k][...]
        keys[k, TOK:, HD:] = jnp.ones((TOK, HD), BF)
    lane = lax.broadcasted_iota(jnp.int32, (TILE, HD), 1)
    lses = [jnp.zeros((TILE, HD), F32) for _ in range(HALVES)]

    def score(job):
        place, h = job
        cols = pl.ds(pl.multiple_of((2 * place + core) * HD, HD), HD)
        scores = dot(query_ref[tile_rows(h), cols], keys[place, :TOK, :HD], ONES)
        return jnp.where(seq > 0, scores, MASKED)

    def finish(job, scores):
        place, h = job
        if job == (0, 0):
            copy.wait()
        column = member * 4 + place
        own_peak = peak_ref[tile_rows(h), column : column + 1]
        own_total = total_ref[tile_rows(h), column : column + 1]
        peak = jnp.maximum(jnp.max(scores, axis=1, keepdims=True), own_peak)
        weights = jnp.exp2(scores * TO_TWO - peak * TO_TWO).astype(BF)
        mixed = dot(weights, keys[place, TOK:, :])
        keep = jnp.exp2((own_peak - peak) * TO_TWO)
        total = mixed[:, HD:] + keep * own_total
        out = (mixed[:, :HD] + keep * acc_ref[place, tile_rows(h), :]) / total
        out_ref[tile_rows(h), place * HD : place * HD + HD] = out.astype(BF)
        lses[h] = jnp.where(lane == place, peak * SCALE + jnp.log(total), lses[h])

    pipelined([(p, h) for p in range(4) for h in range(HALVES)], score, finish)
    for h in range(HALVES):
        lse_ref[:, tile_rows(h)] = lses[h].T[:4]


def back_call(member, where, query, pieces, acc, peak, total):
    whole = pl.BlockSpec(memory_space=pltpu.VMEM)

    def kernel(*refs):
        back_kernel(member, *refs)

    return pl.pallas_call(
        kernel,
        out_shape=(
            jax.ShapeDtypeStruct((TOK, 4 * HD), BF),
            jax.ShapeDtypeStruct((4, TOK), F32),
        ),
        in_specs=[pl.BlockSpec(memory_space=pltpu.SMEM)] + [whole] * 5
        + [pl.BlockSpec(memory_space=pl.ANY), whole, whole],
        out_specs=(whole,) * 2,
        scratch_shapes=[
            pltpu.VMEM((4, 2 * TOK, 2 * HD), BF),
            pltpu.VMEM((4, TOK, HD), F32),
            pltpu.SemaphoreType.DMA,
        ],
        compiler_params=pltpu.CompilerParams(vmem_limit_bytes=14 * 2**20),
        cost_estimate=pl.CostEstimate(
            flops=10**11, bytes_accessed=4 * 2**20, transcendentals=2 * 2**20
        ),
        name="back",
    )(where, query, *pieces, acc, peak, total)


def merge_kernel(where_ref, mine_ref, got_ref, mine_lse, got_lse, out_ref, lse_ref):
    core = where_ref[2]
    for k in range(4):
        cols = slice(k * HD, k * HD + HD)
        at = pl.ds(pl.multiple_of((2 * k + core) * HD, HD), HD)
        out_ref[:, at] = mine_ref[:, cols]
        lse_ref[pl.ds(2 * k + core, 1), :] = mine_lse[k : k + 1, :]
        at = pl.ds(pl.multiple_of((2 * k + 1 - core) * HD, HD), HD)
        out_ref[:, at] = got_ref[:, cols]
        lse_ref[pl.ds(2 * k + 1 - core, 1), :] = got_lse[k : k + 1, :]


def merge_call(where, mine, got, mine_lse, got_lse):
    whole = pl.BlockSpec(memory_space=pltpu.VMEM)
    return pl.pallas_call(
        merge_kernel,
        out_shape=(
            jax.ShapeDtypeStruct((TOK, KVH * HD), BF),
            jax.ShapeDtypeStruct((KVH, TOK), F32),
        ),
        in_specs=[pl.BlockSpec(memory_space=pltpu.SMEM)] + [whole] * 4,
        out_specs=(whole, whole),
        compiler_params=pltpu.CompilerParams(vmem_limit_bytes=14 * 2**20),
        cost_estimate=pl.CostEstimate(flops=0, bytes_accessed=2 * 2**20, transcendentals=0),
        name="merge",
    )(where, mine, got, mine_lse, got_lse)


def one_line(x, moves):
    pairs = [(2 * i + core, 2 * j + core) for i, j in moves for core in range(2)]
    return lax.ppermute(x, "chan", pairs)


def gather_near(x):
    below = one_line(x, [(0, 1), (1, 2), (2, 3)])
    above = one_line(x, [(1, 0), (2, 1), (3, 2)])
    across = one_line(x, [(0, 2), (1, 3), (2, 0), (3, 1)])
    return [x, below, above, across]


def around(x, chips):
    return one_line(x, [(i, (i + chips) % 4) for i in range(4)])


def gather_far(across):
    return one_line(across, [(2, 3), (1, 0)])


def to_next(x):
    pairs = [
        (s * CHAN + c, (s + 1) * CHAN + (c if s % 4 != 3 else 2 * (3 - c // 2) + c % 2))
        for s in range(SEQ - 1)
        for c in range(CHAN)
    ]
    return lax.ppermute(x, ("seq", "chan"), pairs)


def swap(x):
    return lax.ppermute(x, "chan", [(c, c ^ 1) for c in range(CHAN)])


def exchange(x):
    return lax.all_to_all(x, "seq", split_axis=0, concat_axis=0, tiled=True)


def local(
    hyena_gate, hyena_key, hyena_value, long_filter, skip_weight, attn_query, attn_keys, attn_values
):
    seq, chan = lax.axis_index("seq"), lax.axis_index("chan")
    where = jnp.stack([seq, chan // 2, chan % 2]).astype(jnp.int32)
    query = attn_query.reshape(TOK, KVH * HD)
    kv = pack_call(attn_keys, attn_values)
    given_query, kv_ready = lax.optimization_barrier((query, kv))
    query_got = swap(given_query)
    kv_behind = to_next(kv)
    own = gather_near(kv)
    turned = turn_call(hyena_key, hyena_value, long_filter, kv)
    across, _, kv_behind = lax.optimization_barrier((own[3], turned, kv_behind))
    own.append(gather_far(across))
    received = exchange(turned.reshape(2 * SEQ, MINE, TOK)).reshape(SEQ, 2, MINE, TOK)
    mine_acc, given_acc, peak, total = own_call(where, query, query_got, own)
    kv_behind, peak = lax.optimization_barrier((kv_behind, peak))
    behind = [kv_behind] + [around(kv_behind, k) for k in (1, 2, 3)]
    received, peak = lax.optimization_barrier((received, peak))
    conv = conv_call(received)
    placed = exchange(conv)
    given, given_lse = back_call(1, where, query_got, behind, given_acc, peak, total)
    got, got_lse = swap(given), swap(given_lse)
    mine, mine_lse = back_call(0, where, query, behind, mine_acc, peak, total)
    hyena_out = gate_call(
        placed.reshape(CH, TOK), hyena_gate, hyena_key, hyena_value, skip_weight.reshape(1, CH)
    )
    attn_out, attn_lse = merge_call(where, mine, got, mine_lse, got_lse)
    return (
        hyena_out,
        attn_out.reshape(TOK, 1, KVH * HD),
        attn_lse.reshape(1, KVH, TOK),
    )


def solution(mesh):
    return jax.shard_map(
        local,
        mesh=mesh,
        in_specs=(
            P("seq", "chan"),
            P("seq", "chan"),
            P("seq", "chan"),
            P("seq", "chan"),
            P("chan"),
            P("seq", "chan", None),
            P("seq", "chan"),
            P("seq", "chan"),
        ),
        out_specs=(P("seq", "chan"), P("seq", "chan", None), P("chan", None, "seq")),
        check_vma=False,
    )
```
